512 devices in a mesh: space: 64 (over x_lo, z, core), probe: 8 (over x_hi, y).
Axes of the slice: x: 4 (x_hi: 2, x_lo: 2; x = x_hi * 2 + x_lo), y: 4, z: 16, core: 2. Of those that a mesh axis runs over, the one named last changes fastest.
Arguments:
- site_class: int32 [10, 192, 2, 128], P(None, 'space'), may hold values from 0 to 127, as said below
- probe_signs: int32 [30, 32, 192, 2, 128], P(None, 'probe', 'space'), may hold values from 0 to 1
- masses: float32 [128], replicated, may hold values from 1 to 4
- force_blocks: float32 [27, 30, 30], replicated, may hold values from -0.018 to 0.518, as said below
Outputs:
- moments: float32 [4, 128], replicated
- last_term: float32 [30, 32, 192, 2, 128], P(None, 'probe', 'space')
The draws below stay inside these ranges and needn't reach their ends.
Inputs may be any that keep to these rules, and one draw needn't show every extreme that they name: `site_class`: an atom in a cell with first index x has a class in the window of 4 classes that starts at (x // 3) * 2, taken modulo 128. force_blocks[26 - o] is the transpose of force_blocks[o] for every offset index o.
All inputs are finite; a program needn't handle non-finite values.
Results may differ from the reference program's by a relative error of at most 0.00012.
Values sent between devices are 32-bit elements; how exact they have to be, the bound alone decides.
No kernel may reach another device: no remote copies, remote signals or barrier semaphores. Data moves between devices by JAX's collectives and lax.ppermute only.
A program may use at most 64 MiB of HBM per device.

```python
import math
import jax
import jax.numpy as jnp
from jax import lax

ATOMS_CELL = 10
ATOM_COMP = 30
NCLASS = 128
STEPS = 3
PROBES = 32
CX = 3
NY = 2
NZ = 128
NX = 192
CLASS_STRIDE = 2


def draw_site_class(key, part):
    shape = (ATOMS_CELL, NX, NY, NZ)
    tile_index = lax.broadcasted_iota(jnp.int32, shape, 1) // CX
    offsets = jax.random.randint(key, shape, 0, 2 * CLASS_STRIDE)
    return (tile_index * CLASS_STRIDE + offsets) % NCLASS


def draw_force_blocks(key, part):
    shape = (27, ATOM_COMP, ATOM_COMP)
    drawn_values = jnp.clip(0.006 * jax.random.normal(key, shape, jnp.float32), -0.018, 0.018)
    mirrored = jnp.transpose(jnp.flip(drawn_values, 0), (0, 2, 1))
    center = 0.5 * (drawn_values + jnp.transpose(drawn_values, (0, 2, 1))) + 0.5 * jnp.eye(ATOM_COMP, dtype=jnp.float32)
    offset_index = lax.broadcasted_iota(jnp.int32, shape, 0)
    return jnp.where(offset_index < 13, drawn_values, jnp.where(offset_index > 13, mirrored, center))


def set_ends(array, rng, least, largest):
    longest = array.shape.index(max(array.shape))
    spots = []
    for shift in (0, 1):
        where = [jax.random.randint(jax.random.fold_in(rng, axis), (), 0, length) for axis, length in enumerate(array.shape)]
        where[longest] = (where[longest] + shift) % array.shape[longest]
        spots.append(tuple(where))
    return array.at[spots[0]].set(least).at[spots[1]].set(largest)


def setup_inputs(seed: int = 0) -> dict:
    key_of = jax.random.split(jax.random.key(seed), 5)
    site_class = draw_site_class(jax.random.fold_in(key_of[4], 71), 0)
    probe_signs = set_ends(jax.random.randint(key_of[1], (ATOM_COMP, PROBES, NX, NY, NZ), 0, 2), jax.random.fold_in(key_of[1], 1), 0, 1).astype(jnp.int32)
    masses = jnp.clip(jnp.exp(jax.random.uniform(key_of[2], (NCLASS,), jnp.float32, math.log(1.0), math.log(4.0))), 1.0, 4.0)
    force_blocks = draw_force_blocks(jax.random.fold_in(key_of[4], 71), 0)
    return {"site_class": site_class, "probe_signs": probe_signs, "masses": masses, "force_blocks": force_blocks}


exact_mode = lax.Precision.HIGHEST

def stencil_apply(field, force_blocks):
    accumulated = jnp.zeros_like(field)
    for offset in range(27):
        shift_x = offset // 9 - 1
        shift_y = offset // 3 % 3 - 1
        shift_z = offset % 3 - 1
        shifted = jnp.roll(field, (-shift_x, -shift_y, -shift_z), axis=(1, 2, 3))
        accumulated = accumulated + jnp.einsum('ab,bxyz->axyz', force_blocks[offset], shifted, precision=exact_mode)
    return accumulated

def reference(site_class, probe_signs, masses, force_blocks):
    inv_root = 1.0 / jnp.sqrt(masses)
    atom_scale = inv_root[site_class]
    comp_scale = jnp.repeat(atom_scale, 3, axis=0)

    def probe_pass(carry, signs):
        first_term = (2 * signs - 1).astype(jnp.float32)
        second_term = comp_scale * stencil_apply(comp_scale * first_term, force_blocks)
        third_term = 2.0 * (comp_scale * stencil_apply(comp_scale * second_term, force_blocks)) - first_term
        last_term = 2.0 * (comp_scale * stencil_apply(comp_scale * third_term, force_blocks)) - second_term
        products = jnp.stack([first_term * first_term, first_term * second_term, first_term * third_term, first_term * last_term])
        per_atom = products.reshape(STEPS + 1, ATOMS_CELL, 3, -1).sum(axis=2)
        return (carry + per_atom, last_term)
    start = jnp.zeros((STEPS + 1, ATOMS_CELL, NX * NY * NZ), jnp.float32)
    per_atom, last_terms = lax.scan(probe_pass, start, jnp.moveaxis(probe_signs, 1, 0))
    labels = site_class.reshape(-1)
    sums = jax.ops.segment_sum(per_atom.reshape(STEPS + 1, -1).T, labels, num_segments=NCLASS).T
    scale = 1.0 / (PROBES * ATOM_COMP * CX * NY * NZ / CLASS_STRIDE)
    return (sums * scale, jnp.moveaxis(last_terms, 0, 1))
```

```python
import jax
import jax.numpy as jnp
from jax import lax
from jax.experimental import pallas as pl
from jax.experimental.pallas import tpu as pltpu
from jax.sharding import Mesh, PartitionSpec as P

SPACE = ("xl", "z", "core")
PROBE = ("xh", "y")
NEAR = ("xl", "core", "xh", "y")

COMP, PAD = 30, 32
ATOMS, ATOM_PAD = 10, 16
NP, CX, NY, NZ = 4, 3, 2, 128
PLANES = 3 * CX
ROWS = NY * PAD
WIDE = NP * NZ
SIGN_ROWS = CX * NY * NP * PAD
PAY_ROWS = SIGN_ROWS + CX * NY * ATOM_PAD
WIN = 4


def weight_kernel(fb_ref, hi_ref, lo_ref, full):
    full[...] = jnp.zeros_like(full)
    for dx in range(3):
        for dz in range(3):
            same = fb_ref[9 * dx + 3 + dz]
            other = fb_ref[9 * dx + dz] + fb_ref[9 * dx + 6 + dz]
            for y in range(NY):
                for y2 in range(NY):
                    r, c = dz * ROWS + y * PAD, dx * ROWS + y2 * PAD
                    full[r : r + COMP, c : c + COMP] = same if y == y2 else other
    hi = full[...].astype(jnp.bfloat16)
    hi_ref[...] = hi
    lo_ref[...] = (full[...] - hi.astype(jnp.float32)).astype(jnp.bfloat16)


def main_kernel(mass_ref, own_ref, a_ref, b_ref, wh_ref, wl_ref, out_ref, pm_ref, uh, ul, v0s, v1s, ss, rels):
    core = lax.axis_index("core")
    idx = (lax.axis_index("xl") * lax.axis_size("z") + lax.axis_index("z")) * 2 + core
    is_even = core == 0

    def rows(slab, start, count):
        where = slice(start, start + count)
        if slab == 1:
            return own_ref[where, :]
        near, far = a_ref[where, :], b_ref[where, :]
        return jnp.where(is_even, far, near) if slab == 0 else jnp.where(is_even, near, far)

    spread = (
        lax.broadcasted_iota(jnp.int32, (PAD, ATOM_PAD), 0) // 3
        == lax.broadcasted_iota(jnp.int32, (PAD, ATOM_PAD), 1)
    ).astype(jnp.bfloat16)
    valid = lax.broadcasted_iota(jnp.int32, (PAD, NZ), 0) < COMP

    for slab in range(3):
        base = 2 * ((idx + slab - 1) & 63)
        inv = [1.0 / jnp.sqrt(jnp.full((1, NZ), mass_ref[(base + j) & 127], jnp.float32)) for j in range(WIN)]
        labels = jnp.concatenate(
            [rows(slab, SIGN_ROWS + i * ATOM_PAD, ATOM_PAD) for i in range(CX * NY)], axis=1
        )
        labels = jnp.dot(spread, labels.astype(jnp.float32).astype(jnp.bfloat16), preferred_element_type=jnp.float32)
        rel = (labels.astype(jnp.int32) - base) & 127
        for x in range(CX):
            for y in range(NY):
                i = x * NY + y
                part = rel[:, i * NZ : (i + 1) * NZ]
                scale = jnp.where(part == 0, inv[0], jnp.where(part == 1, inv[1], jnp.where(part == 2, inv[2], inv[3])))
                scale = jnp.where(valid, scale, 0.0)
                at = (slab * CX + x) * ROWS + y * PAD
                ss[at : at + PAD, :] = scale
                if slab == 1:
                    rels[i * PAD : (i + 1) * PAD, :] = jnp.where(valid, part, -1)
                for p in range(NP):
                    sign = rows(slab, (i * NP + p) * PAD, PAD)
                    v0 = (2 * sign - 1).astype(jnp.float32)
                    lanes = slice(p * NZ, (p + 1) * NZ)
                    v0s[at : at + PAD, lanes] = v0
                    u = scale * v0
                    hi = u.astype(jnp.bfloat16)
                    uh[0, at : at + PAD, lanes] = hi
                    ul[0, at : at + PAD, lanes] = (u - hi.astype(jnp.float32)).astype(jnp.bfloat16)

    wh, wl = wh_ref[...], wl_ref[...]
    sums = [[jnp.zeros((8, NZ), jnp.float32) for _ in range(WIN)] for _ in range(4)]

    def add_moments(n, plane, total):
        for j in range(WIN):
            mask = rels[(plane - CX) * ROWS : (plane - CX + 1) * ROWS, :] == j
            picked = jnp.where(mask, total, 0.0)
            sums[n][j] = sums[n][j] + sum(picked[8 * k : 8 * k + 8] for k in range(ROWS // 8))

    for step in range(3):
        for plane in range(step + 1, PLANES - 1 - step):
            here = slice(plane * ROWS, (plane + 1) * ROWS)
            around = slice((plane - 1) * ROWS, (plane + 2) * ROWS)
            scale = ss[here, :]
            inner = CX <= plane < 2 * CX
            total = jnp.zeros((ROWS, NZ), jnp.float32)
            if inner and step == 0:
                count = sum(v0s[here, p * NZ : (p + 1) * NZ] * v0s[here, p * NZ : (p + 1) * NZ] for p in range(NP))
                add_moments(0, plane, count)
            for pair in range(NP // 2):
                wide = slice(pair * 2 * NZ, (pair + 1) * 2 * NZ)
                high, low = uh[step, around, wide], ul[step, around, wide]
                t = (
                    jnp.dot(wh, high, preferred_element_type=jnp.float32)
                    + jnp.dot(wh, low, preferred_element_type=jnp.float32)
                    + jnp.dot(wl, high, preferred_element_type=jnp.float32)
                )
                for q in range(2):
                    lanes = slice((pair * 2 + q) * NZ, (pair * 2 + q + 1) * NZ)
                    col = slice(q * NZ, (q + 1) * NZ)
                    g = (
                        pltpu.roll(t[0:ROWS, col], 1, 1)
                        + t[ROWS : 2 * ROWS, col]
                        + pltpu.roll(t[2 * ROWS :, col], NZ - 1, 1)
                    ) * scale
                    v0 = v0s[here, lanes]
                    if step == 0:
                        v = g
                        v1s[here, lanes] = v
                    elif step == 1:
                        v = 2.0 * g - v0
                    else:
                        v = 2.0 * g - v1s[here, lanes]
                        out_ref[plane - CX, :, lanes] = v
                    if step < 2:
                        u = scale * v
                        hi = u.astype(jnp.bfloat16)
                        uh[step + 1, here, lanes] = hi
                        ul[step + 1, here, lanes] = (u - hi.astype(jnp.float32)).astype(jnp.bfloat16)
                    if inner:
                        total = total + v0 * v
            if inner:
                add_moments(step + 1, plane, total)

    lane = lax.broadcasted_iota(jnp.int32, (4, NZ), 1)
    moments = jnp.zeros((4, NZ), jnp.float32)
    for j in range(WIN):
        stacked = jnp.concatenate([jnp.sum(sums[n][j], axis=0, keepdims=True) for n in range(4)], axis=0)
        value = jnp.sum(stacked, axis=1, keepdims=True)
        moments = moments + jnp.where(lane == ((2 * idx + j) & 127), value, 0.0)
    pm_ref[...] = jnp.broadcast_to(moments[None], pm_ref.shape)


VMEM = pl.BlockSpec(memory_space=pltpu.VMEM)
SMEM = pl.BlockSpec(memory_space=pltpu.SMEM)


def body(site_class, probe_signs, masses, force_blocks):
    signs = jnp.transpose(probe_signs, (2, 3, 1, 0, 4))
    signs = jnp.pad(signs, ((0, 0),) * 3 + ((0, PAD - COMP), (0, 0))).reshape(SIGN_ROWS, NZ)
    labels = jnp.transpose(site_class, (1, 2, 0, 3))
    labels = jnp.pad(labels, ((0, 0),) * 2 + ((0, ATOM_PAD - ATOMS), (0, 0))).reshape(-1, NZ)
    payload = jnp.concatenate([signs, labels], axis=0)

    count = 64
    far = lax.ppermute(payload, SPACE, [(i, (i + 1) % count if i % 2 else (i - 1) % count) for i in range(count)])
    near = lax.ppermute(payload, SPACE, [(i, i ^ 1) for i in range(count)])

    wide = 3 * ROWS
    high, low = pl.pallas_call(
        weight_kernel,
        out_shape=(jax.ShapeDtypeStruct((wide, wide), jnp.bfloat16),) * 2,
        in_specs=[VMEM],
        out_specs=(VMEM, VMEM),
        scratch_shapes=[pltpu.VMEM((wide, wide), jnp.float32)],
        cost_estimate=pl.CostEstimate(flops=1000000, bytes_accessed=300000, transcendentals=0),
        name="weights",
    )(force_blocks)

    group = 32
    last, parts = pl.pallas_call(
        main_kernel,
        out_shape=(
            jax.ShapeDtypeStruct((CX, ROWS, WIDE), jnp.float32),
            jax.ShapeDtypeStruct((group, 4, NZ), jnp.float32),
        ),
        in_specs=[SMEM] + [VMEM] * 5,
        out_specs=(VMEM, VMEM),
        scratch_shapes=[
            pltpu.VMEM((3, PLANES * ROWS, WIDE), jnp.bfloat16),
            pltpu.VMEM((3, PLANES * ROWS, WIDE), jnp.bfloat16),
            pltpu.VMEM((PLANES * ROWS, WIDE), jnp.float32),
            pltpu.VMEM((PLANES * ROWS, WIDE), jnp.float32),
            pltpu.VMEM((PLANES * ROWS, NZ), jnp.float32),
            pltpu.VMEM((CX * ROWS, NZ), jnp.int32),
        ],
        compiler_params=pltpu.CompilerParams(vmem_limit_bytes=40 * 2**20),
        cost_estimate=pl.CostEstimate(flops=2000000000, bytes_accessed=2000000, transcendentals=0),
        name="chebyshev",
    )(masses, payload, near, far, high, low)

    parts = lax.all_to_all(parts, NEAR, 0, 0, tiled=True).sum(0)
    parts = jnp.broadcast_to(parts[None], (lax.axis_size("z"), 4, NZ))
    moments = lax.all_to_all(parts, "z", 0, 0, tiled=True).sum(0) * (1.0 / 368640)

    last = last.reshape(CX, NY, PAD, NP, NZ)[:, :, :COMP]
    return moments, jnp.transpose(last, (2, 3, 0, 1, 4))


def solution(mesh):
    fine = Mesh(mesh.devices.reshape(2, 16, 2, 2, 4), SPACE + PROBE)
    return jax.shard_map(
        body,
        mesh=fine,
        in_specs=(P(None, SPACE, None, None), P(None, PROBE, SPACE, None, None), P(), P()),
        out_specs=(P(), P(None, PROBE, SPACE, None, None)),
        check_vma=False,
    )
```

```python
import jax
import jax.numpy as jnp
from jax import lax
from jax.experimental import pallas as pl
from jax.experimental.pallas import tpu as pltpu
from jax.sharding import Mesh, PartitionSpec as P

SPACE = ("xl", "z", "core")
PROBE = ("xh", "y")
NEAR = ("xl", "core", "xh", "y")

COMP, PAD = 30, 32
ATOMS, ATOM_PAD = 10, 16
NP, CX, NY, NZ = 4, 3, 2, 128
PLANES = 3 * CX
ROWS = NY * PAD
WIDE = NP * NZ
CELLS = CX * NY
SIGN_ROWS = COMP * NP * CELLS
LABEL_ROWS = ATOMS * CELLS
PAY_ROWS = SIGN_ROWS + LABEL_ROWS
WIN = 4


def split(u):
    hi = u.astype(jnp.bfloat16)
    return hi, (u - hi.astype(jnp.float32)).astype(jnp.bfloat16)


def window_of(idx):
    return 2 * (idx & 63)


def own_index():
    return (lax.axis_index("xl") * lax.axis_size("z") + lax.axis_index("z")) * 2 + lax.axis_index("core")


def load_slab(rows, base, inv, emit):
    spread = (
        lax.broadcasted_iota(jnp.int32, (PAD, ATOM_PAD), 0) // 3
        == lax.broadcasted_iota(jnp.int32, (PAD, ATOM_PAD), 1)
    ).astype(jnp.bfloat16)
    valid = lax.broadcasted_iota(jnp.int32, (PAD, NZ), 0) < COMP
    labels = jnp.concatenate([rows(pl.ds(SIGN_ROWS + i, ATOMS, stride=CELLS)) for i in range(CELLS)], axis=1)
    labels = jnp.concatenate([labels, jnp.zeros((ATOM_PAD - ATOMS, CELLS * NZ), jnp.int32)], axis=0)
    labels = jnp.dot(spread, labels.astype(jnp.float32).astype(jnp.bfloat16), preferred_element_type=jnp.float32)
    rel = (labels.astype(jnp.int32) - base) & 127
    for i in range(CX * NY):
        part = rel[:, i * NZ : (i + 1) * NZ]
        scale = jnp.where(part == 0, inv[0], jnp.where(part == 1, inv[1], jnp.where(part == 2, inv[2], inv[3])))
        scale = jnp.where(valid, scale, 0.0)
        signs = []
        for p in range(NP):
            sign = rows(pl.ds(p * CELLS + i, COMP, stride=NP * CELLS))
            sign = jnp.concatenate([sign, jnp.zeros((PAD - COMP, NZ), jnp.int32)], axis=0)
            signs.append((2 * sign - 1).astype(jnp.float32))
        emit(slice(i * PAD, (i + 1) * PAD), scale, jnp.where(valid, part, -1), signs)


def payload_kernel(signs_ref, labels_ref, pay_ref, sems):
    copies = [
        pltpu.make_async_copy(signs_ref.reshape(SIGN_ROWS, NZ), pay_ref.at[0:SIGN_ROWS, :], sems.at[0]),
        pltpu.make_async_copy(labels_ref.reshape(LABEL_ROWS, NZ), pay_ref.at[SIGN_ROWS : SIGN_ROWS + LABEL_ROWS, :], sems.at[1]),
    ]
    for copy in copies:
        copy.start()
    for copy in copies:
        copy.wait()


def prepare_kernel(mass_ref, fb_ref, own_ref, w_ref, inv_ref, uh_ref, ul_ref, v0_ref, s_ref, rel_ref, full):
    full[...] = jnp.zeros_like(full)
    for dx in range(3):
        for dz in range(3):
            same = fb_ref[9 * dx + 3 + dz]
            other = fb_ref[9 * dx + dz] + fb_ref[9 * dx + 6 + dz]
            for y in range(NY):
                for y2 in range(NY):
                    r, c = dz * ROWS + y * PAD, dx * ROWS + y2 * PAD
                    full[r : r + COMP, c : c + COMP] = same if y == y2 else other
    w_ref[0 : 3 * ROWS, :], w_ref[3 * ROWS :, :] = split(full[...])

    idx = own_index()
    inv = []
    for slab in range(3):
        base = window_of(idx + slab - 1)
        row = [1.0 / jnp.sqrt(jnp.full((1, NZ), mass_ref[(base + j) & 127], jnp.float32)) for j in range(WIN)]
        inv.append(row)
        if slab != 1:
            for j in range(WIN):
                at = slab * 2 + j
                inv_ref[at : at + 1, :] = row[j]

    def emit(at, scale, rel, signs):
        s_ref[at, :] = scale
        rel_ref[at, :] = rel
        for p, v0 in enumerate(signs):
            lanes = slice(p * NZ, (p + 1) * NZ)
            v0_ref[at, lanes] = v0
            uh_ref[at, lanes], ul_ref[at, lanes] = split(scale * v0)

    load_slab(lambda at: own_ref[at, :], window_of(idx), inv[1], emit)


def main_kernel(
    a_ref, b_ref, w_ref, inv_ref, uh_ref, ul_ref, v0_ref, s_ref, rel_ref, out_ref, pm_ref, uh, ul, v0s, v1s, ss, result, sem
):
    idx = own_index()
    is_even = lax.axis_index("core") == 0
    own = slice(CX * ROWS, 2 * CX * ROWS)
    uh[0, own, :] = uh_ref[...]
    ul[0, own, :] = ul_ref[...]

    for slab in (0, 2):

        def rows(at, slab=slab):
            near, far = a_ref[at, :], b_ref[at, :]
            return jnp.where(is_even, far, near) if slab == 0 else jnp.where(is_even, near, far)

        def emit(at, scale, rel, signs, slab=slab):
            at = slice(at.start + slab * CX * ROWS, at.stop + slab * CX * ROWS)
            ss[at, :] = scale
            for p, v0 in enumerate(signs):
                lanes = slice(p * NZ, (p + 1) * NZ)
                v0s[at, lanes] = v0
                uh[0, at, lanes], ul[0, at, lanes] = split(scale * v0)

        inv = [inv_ref[slab * 2 + j : slab * 2 + j + 1, :] for j in range(WIN)]
        load_slab(rows, window_of(idx + slab - 1), inv, emit)

    weights = w_ref[...]
    high_weights = w_ref[0 : 3 * ROWS, :]
    sums = [[jnp.zeros((8, NZ), jnp.float32) for _ in range(WIN)] for _ in range(4)]

    def add_moments(n, inner, total):
        for j in range(WIN):
            picked = jnp.where(rel_ref[inner, :] == j, total, 0.0)
            sums[n][j] = sums[n][j] + sum(picked[8 * k : 8 * k + 8] for k in range(ROWS // 8))

    writes = []
    for step in range(3):
        for plane in range(step + 1, PLANES - 1 - step):
            here = slice(plane * ROWS, (plane + 1) * ROWS)
            around = slice((plane - 1) * ROWS, (plane + 2) * ROWS)
            is_own = CX <= plane < 2 * CX
            inner = slice((plane - CX) * ROWS, (plane - CX + 1) * ROWS)
            scale = s_ref[inner, :] if is_own else ss[here, :]
            total = jnp.zeros((ROWS, NZ), jnp.float32)
            if is_own and step == 0:
                first = [v0_ref[inner, p * NZ : (p + 1) * NZ] for p in range(NP)]
                add_moments(0, inner, sum(v * v for v in first))
            for pair in range(NP // 2):
                wide = slice(pair * 2 * NZ, (pair + 1) * 2 * NZ)
                both = jnp.dot(weights, uh[step, around, wide], preferred_element_type=jnp.float32)
                low = jnp.dot(high_weights, ul[step, around, wide], preferred_element_type=jnp.float32)
                t = both[0 : 3 * ROWS] + (both[3 * ROWS :] + low)
                for q in range(2):
                    p = pair * 2 + q
                    lanes = slice(p * NZ, (p + 1) * NZ)
                    col = slice(q * NZ, (q + 1) * NZ)
                    g = (
                        pltpu.roll(t[0:ROWS, col], 1, 1)
                        + t[ROWS : 2 * ROWS, col]
                        + pltpu.roll(t[2 * ROWS :, col], NZ - 1, 1)
                    ) * scale
                    v0 = v0_ref[inner, lanes] if is_own else v0s[here, lanes]
                    if step == 0:
                        v = g
                        v1s[here, lanes] = v
                    elif step == 1:
                        v = 2.0 * g - v0
                    else:
                        v = 2.0 * g - v1s[here, lanes]
                        for y in range(NY):
                            result[plane - CX, pl.ds(p * NY + y, COMP, stride=NP * NY), :] = v[y * PAD : y * PAD + COMP]
                    if step < 2:
                        uh[step + 1, here, lanes], ul[step + 1, here, lanes] = split(scale * v)
                    if is_own:
                        total = total + v0 * v
            if step == 2:
                x = plane - CX
                writes.append(pltpu.make_async_copy(result.at[x].reshape(COMP * NP, NY, NZ), out_ref.at[:, x], sem.at[x]))
                writes[x].start()
            if is_own:
                add_moments(step + 1, inner, total)

    lane = lax.broadcasted_iota(jnp.int32, (4, NZ), 1)
    moments = jnp.zeros((4, NZ), jnp.float32)
    for j in range(WIN):
        stacked = jnp.concatenate([jnp.sum(sums[n][j], axis=0, keepdims=True) for n in range(4)], axis=0)
        value = jnp.sum(stacked, axis=1, keepdims=True)
        moments = moments + jnp.where(lane == ((window_of(idx) + j) & 127), value, 0.0)
    pm_ref[...] = jnp.broadcast_to(moments[None], pm_ref.shape)
    for write in writes:
        write.wait()


HBM = pl.BlockSpec(memory_space=pltpu.HBM)
VMEM = pl.BlockSpec(memory_space=pltpu.VMEM)
SMEM = pl.BlockSpec(memory_space=pltpu.SMEM)


def body(site_class, probe_signs, masses, force_blocks):
    payload = pl.pallas_call(
        payload_kernel,
        out_shape=pltpu.VMEM((PAY_ROWS, NZ), jnp.int32),
        in_specs=[HBM, HBM],
        out_specs=VMEM,
        scratch_shapes=[pltpu.SemaphoreType.DMA((2,))],
        cost_estimate=pl.CostEstimate(flops=0, bytes_accessed=800000, transcendentals=0),
        name="payload",
    )(probe_signs.reshape(COMP * NP * CX, NY, NZ), site_class.reshape(ATOMS * CX, NY, NZ))

    count = 64
    far = lax.ppermute(payload, SPACE, [(i, (i + 1) % count if i % 2 else (i - 1) % count) for i in range(count)])
    near = lax.ppermute(payload, SPACE, [(i, i ^ 1) for i in range(count)])

    prepared = pl.pallas_call(
        prepare_kernel,
        out_shape=(
            pltpu.VMEM((6 * ROWS, 3 * ROWS), jnp.bfloat16),
            pltpu.VMEM((8, NZ), jnp.float32),
            pltpu.VMEM((CX * ROWS, WIDE), jnp.bfloat16),
            pltpu.VMEM((CX * ROWS, WIDE), jnp.bfloat16),
            pltpu.VMEM((CX * ROWS, WIDE), jnp.float32),
            pltpu.VMEM((CX * ROWS, NZ), jnp.float32),
            pltpu.VMEM((CX * ROWS, NZ), jnp.int32),
        ),
        in_specs=[SMEM, VMEM, VMEM],
        out_specs=(VMEM,) * 7,
        scratch_shapes=[pltpu.VMEM((3 * ROWS, 3 * ROWS), jnp.float32)],
        cost_estimate=pl.CostEstimate(flops=1000000, bytes_accessed=300000, transcendentals=0),
        name="prepare",
    )(masses, force_blocks, payload)

    group = 32
    last, parts = pl.pallas_call(
        main_kernel,
        out_shape=(
            jax.ShapeDtypeStruct((COMP * NP, CX, NY, NZ), jnp.float32),
            jax.ShapeDtypeStruct((group, 4, NZ), jnp.float32),
        ),
        in_specs=[VMEM] * 9,
        out_specs=(pl.BlockSpec(memory_space=pltpu.HBM), VMEM),
        scratch_shapes=[
            pltpu.VMEM((3, PLANES * ROWS, WIDE), jnp.bfloat16),
            pltpu.VMEM((3, PLANES * ROWS, WIDE), jnp.bfloat16),
            pltpu.VMEM((PLANES * ROWS, WIDE), jnp.float32),
            pltpu.VMEM((PLANES * ROWS, WIDE), jnp.float32),
            pltpu.VMEM((PLANES * ROWS, NZ), jnp.float32),
            pltpu.VMEM((CX, SIGN_ROWS // CX, NZ), jnp.float32),
            pltpu.SemaphoreType.DMA((CX,)),
        ],
        compiler_params=pltpu.CompilerParams(vmem_limit_bytes=24 * 2**20),
        cost_estimate=pl.CostEstimate(flops=2000000000, bytes_accessed=2000000, transcendentals=0),
        name="chebyshev",
    )(near, far, *prepared)

    parts = lax.all_to_all(parts, NEAR, 0, 0, tiled=True).sum(0)
    parts = jnp.broadcast_to(parts[None], (lax.axis_size("z"), 4, NZ))
    moments = lax.all_to_all(parts, "z", 0, 0, tiled=True).sum(0) * (1.0 / 368640)
    return moments, last.reshape(COMP, NP, CX, NY, NZ)


def solution(mesh):
    fine = Mesh(mesh.devices.reshape(2, 16, 2, 2, 4), SPACE + PROBE)
    return jax.shard_map(
        body,
        mesh=fine,
        in_specs=(P(None, SPACE, None, None), P(None, PROBE, SPACE, None, None), P(), P()),
        out_specs=(P(), P(None, PROBE, SPACE, None, None)),
        check_vma=False,
    )
```

```python
import jax
import jax.numpy as jnp
from jax import lax
from jax.experimental import pallas as pl
from jax.experimental.pallas import tpu as pltpu
from jax.sharding import Mesh, PartitionSpec as P

SPACE = ("xl", "z", "core")
PROBE = ("xh", "y")
NEAR = ("xl", "core", "xh", "y")

COMP, PAD = 30, 32
ATOMS, ATOM_PAD = 10, 16
NP, CX, NY, NZ = 4, 3, 2, 128
CELLS = CX * NY
ROWS = NY * PAD
WIDE = NP * NZ
SIGN_ROWS = COMP * NP * CELLS
LABEL_ROWS = ATOMS * CELLS
PAY_ROWS = SIGN_ROWS + LABEL_ROWS
PAY_PAD = PAY_ROWS + 4
WIN = 4
BAND = 3 * PAD
HALF = (2, 2)


def split(u):
    hi = u.astype(jnp.bfloat16)
    return hi, (u - hi.astype(jnp.float32)).astype(jnp.bfloat16)


def window_of(idx):
    return 2 * (idx & 63)


def own_index():
    return (lax.axis_index("xl") * lax.axis_size("z") + lax.axis_index("z")) * 2 + lax.axis_index("core")


def turned(k):
    return jnp.where(lax.axis_index("core") == 0, k, 2 - k)


def neighbour(slab):
    return own_index() + jnp.where(lax.axis_index("core") == 0, slab - 1, 1 - slab)


def store_scaled(u_ref, at, lanes, scales, fields):
    first, second = scales[0] * fields[0], scales[1] * fields[1]
    for sign, u in enumerate((first + second, first - second)):
        u_ref[sign, 0, at, lanes], u_ref[sign, 1, at, lanes] = split(u)


def load_slab(pay_ref, base, inv, u_ref, v0_ref, s_ref, rel_ref=None, offset=0):
    spread = (
        lax.broadcasted_iota(jnp.int32, (PAD, ATOM_PAD), 0) // 3
        == lax.broadcasted_iota(jnp.int32, (PAD, ATOM_PAD), 1)
    ).astype(jnp.bfloat16)
    valid = lax.broadcasted_iota(jnp.int32, (PAD, NZ), 0) < COMP
    cell = [turned(i // NY) * NY + i % NY for i in range(CELLS)]
    labels = jnp.concatenate(
        [pay_ref[pl.ds(offset + SIGN_ROWS + cell[i], ATOMS, stride=CELLS), :] for i in range(CELLS)], axis=1
    )
    labels = jnp.concatenate([labels, jnp.zeros((ATOM_PAD - ATOMS, CELLS * NZ), jnp.int32)], axis=0)
    labels = jnp.dot(spread, labels.astype(jnp.float32).astype(jnp.bfloat16), preferred_element_type=jnp.float32)
    rel = (labels.astype(jnp.int32) - base) & 127
    for x in range(CX):
        scales = []
        for y in range(NY):
            i = x * NY + y
            part = rel[:, i * NZ : (i + 1) * NZ]
            scale = jnp.where(part == 0, inv[0], jnp.where(part == 1, inv[1], jnp.where(part == 2, inv[2], inv[3])))
            scales.append(jnp.where(valid, scale, 0.0))
            at = slice(i * PAD, (i + 1) * PAD)
            s_ref[at, :] = scales[y]
            if rel_ref is not None:
                rel_ref[at, :] = jnp.where(valid, part, -1)
        for p in range(NP):
            lanes = slice(p * NZ, (p + 1) * NZ)
            fields = []
            for y in range(NY):
                i = x * NY + y
                sign = pay_ref[pl.ds(offset + p * CELLS + cell[i], COMP, stride=NP * CELLS), :]
                sign = jnp.concatenate([sign, jnp.zeros((PAD - COMP, NZ), jnp.int32)], axis=0)
                fields.append((2 * sign - 1).astype(jnp.float32))
                v0_ref[i * PAD : (i + 1) * PAD, lanes] = fields[y]
            store_scaled(u_ref, slice(x * PAD, (x + 1) * PAD), lanes, scales, fields)


def stencil(w_ref, planes, pair):
    lanes = slice(pair * 2 * NZ, (pair + 1) * 2 * NZ)
    sums = []
    for sign in range(2):
        field = jnp.concatenate(
            [ref[sign, part, at * PAD : (at + 1) * PAD, lanes] for part in range(2) for ref, at in planes], axis=0
        )
        t = jnp.dot(w_ref[sign], field, preferred_element_type=jnp.float32)
        o = t[0:BAND] + t[BAND:]
        sums.append(
            [
                pltpu.roll(o[0:PAD, c], 1, 1) + o[PAD : 2 * PAD, c] + pltpu.roll(o[2 * PAD :, c], NZ - 1, 1)
                for c in (slice(0, NZ), slice(NZ, 2 * NZ))
            ]
        )
    even, odd = sums
    return [(even[q] + odd[q], even[q] - odd[q]) for q in range(2)]


def cell_rows(ref, plane, lanes):
    return [ref[(plane * NY + y) * PAD : (plane * NY + y + 1) * PAD, lanes] for y in range(NY)]


ALL = slice(None)


class Moments:
    def __init__(self, rel_ref, v0_ref):
        self.rel_ref, self.v0_ref, self.sums = rel_ref, v0_ref, {}

    def add(self, n, x, fields):
        rels = cell_rows(self.rel_ref, x, ALL)
        for y in range(NY):
            total = 0.0
            for p, field in enumerate(fields):
                total = total + cell_rows(self.v0_ref, x, slice(p * NZ, (p + 1) * NZ))[y] * field[y]
            for j in range(WIN):
                picked = jnp.where(rels[y] == j, total, 0.0)
                part = sum(picked[8 * k : 8 * k + 8] for k in range(PAD // 8))
                self.sums[n, j] = self.sums[n, j] + part if (n, j) in self.sums else part


def payload_kernel(signs_ref, labels_ref, pay_ref, sems):
    copies = [
        pltpu.make_async_copy(signs_ref.reshape(SIGN_ROWS, NZ), pay_ref.at[0:SIGN_ROWS, :], sems.at[0]),
        pltpu.make_async_copy(labels_ref.reshape(LABEL_ROWS, NZ), pay_ref.at[SIGN_ROWS:PAY_ROWS, :], sems.at[1]),
    ]
    for copy in copies:
        copy.start()
    for copy in copies:
        copy.wait()


def prepare_kernel(mass_ref, fb_ref, own_ref, w_ref, inv_ref, u_ref, v0_ref, s_ref, rel_ref, again_ref, full):
    for k in range(2):
        again_ref[k * PAY_PAD : (k + 1) * PAY_PAD, :] = own_ref[...]
    full[...] = jnp.zeros_like(full)
    for k in range(3):
        dx = turned(k)
        for dz in range(3):
            same = fb_ref[9 * dx + 3 + dz]
            other = fb_ref[9 * dx + dz] + fb_ref[9 * dx + 6 + dz]
            r, c = dz * PAD, k * PAD
            full[0, r : r + COMP, c : c + COMP] = 0.5 * (same + other)
            full[1, r : r + COMP, c : c + COMP] = 0.5 * (same - other)
    for sign in range(2):
        hi, lo = split(full[sign])
        w_ref[sign, 0:BAND, :] = jnp.concatenate([hi[:, 0:BAND], hi[:, 0:BAND]], axis=1)
        w_ref[sign, BAND:, :] = jnp.concatenate([lo[:, 0:BAND], jnp.zeros((BAND, BAND), jnp.bfloat16)], axis=1)

    for slab in range(3):
        base = window_of(neighbour(slab))
        inv = [1.0 / jnp.sqrt(jnp.full((1, NZ), mass_ref[(base + j) & 127], jnp.float32)) for j in range(WIN)]
        if slab == 1:
            load_slab(own_ref, base, inv, u_ref, v0_ref, s_ref, rel_ref)
        else:
            for j in range(WIN):
                at = slab * 2 + j
                inv_ref[at : at + 1, :] = inv[j]


def near_kernel(pay_ref, w_ref, inv_ref, u0, v0, s, rel, u1_ref, u2_ref, v1_ref, sums_ref, u0n, v0n, sn):
    inv = [inv_ref[4 + j : 5 + j, :] for j in range(WIN)]
    offset = (1 - lax.axis_index("core")) * PAY_PAD
    load_slab(pay_ref, window_of(neighbour(2)), inv, u0n, v0n, sn, offset=offset)
    moments = Moments(rel, v0)
    lanes_of = [slice(p * NZ, (p + 1) * NZ) for p in range(NP)]
    for x in range(CX):
        moments.add(0, x, [cell_rows(v0, x, lanes_of[p]) for p in range(NP)])

    def first(plane):
        return (u0, plane - 3) if plane < 6 else (u0n, plane - 6)

    def scales_of(plane):
        return cell_rows(s, plane - 3, ALL) if plane < 6 else cell_rows(sn, plane - 6, ALL)

    for plane in (4, 5, 6, 7):
        scales, fields = scales_of(plane), []
        for pair in range(NP // 2):
            for q, g in enumerate(stencil(w_ref, [first(plane + d) for d in (-1, 0, 1)], pair)):
                lanes = lanes_of[2 * pair + q]
                v = [scales[y] * g[y] for y in range(NY)]
                store_scaled(u1_ref, slice((plane - 4) * PAD, (plane - 3) * PAD), lanes, scales, v)
                fields.append(v)
                if plane < 6:
                    for y in range(NY):
                        at = (plane - 4) * ROWS + y * PAD
                        v1_ref[at : at + PAD, lanes] = v[y]
        if plane < 6:
            moments.add(1, plane - 3, fields)
    for plane in (5, 6):
        scales, fields = scales_of(plane), []
        for pair in range(NP // 2):
            for q, g in enumerate(stencil(w_ref, [(u1_ref, plane - 4 + d) for d in (-1, 0, 1)], pair)):
                lanes = lanes_of[2 * pair + q]
                before = cell_rows(v0, 2, lanes) if plane == 5 else cell_rows(v0n, 0, lanes)
                v = [2.0 * (scales[y] * g[y]) - before[y] for y in range(NY)]
                store_scaled(u2_ref, slice((plane - 5) * PAD, (plane - 4) * PAD), lanes, scales, v)
                fields.append(v)
        if plane == 5:
            moments.add(2, 2, fields)
    for n in range(4):
        for j in range(WIN):
            at = (n * WIN + j) * 8
            sums_ref[at : at + 8, :] = moments.sums.get((n, j), jnp.zeros((8, NZ), jnp.float32))


def far_kernel(
    pay_ref, w_ref, inv_ref, u0, v0, s, rel, u1, u2, v1, sums_ref, out_ref, pm_ref, u0f, v0f, sf, u1f, u2f, v1f
):
    inv = [inv_ref[j : j + 1, :] for j in range(WIN)]
    load_slab(pay_ref, window_of(neighbour(0)), inv, u0f, v0f, sf)
    moments = Moments(rel, v0)
    for n in range(4):
        for j in range(WIN):
            at = (n * WIN + j) * 8
            moments.sums[n, j] = sums_ref[at : at + 8, :]
    lanes_of = [slice(p * NZ, (p + 1) * NZ) for p in range(NP)]

    def source(step, plane):
        if step == 0:
            return (u0f, plane) if plane < 3 else (u0, plane - 3)
        if step == 1:
            return (u1f, plane - 1) if plane < 4 else (u1, plane - 4)
        return (u2f, plane - 2) if plane < 5 else (u2, plane - 5)

    flat = out_ref.reshape(SIGN_ROWS, NZ)
    for step in range(3):
        for plane in range(step + 1, step + 4):
            own = plane >= 3
            scales = cell_rows(s, plane - 3, ALL) if own else cell_rows(sf, plane, ALL)
            fields = []
            for pair in range(NP // 2):
                planes = [source(step, plane + d) for d in (-1, 0, 1)]
                for q, g in enumerate(stencil(w_ref, planes, pair)):
                    p = 2 * pair + q
                    lanes = lanes_of[p]
                    v = [scales[y] * g[y] for y in range(NY)]
                    if step == 1:
                        before = cell_rows(v0, plane - 3, lanes) if own else cell_rows(v0f, plane, lanes)
                        v = [2.0 * v[y] - before[y] for y in range(NY)]
                    elif step == 2:
                        before = cell_rows(v1f, 0, lanes) if plane == 3 else cell_rows(v1, plane - 4, lanes)
                        v = [2.0 * v[y] - before[y] for y in range(NY)]
                    if step == 0 and own:
                        for y in range(NY):
                            v1f[y * PAD : (y + 1) * PAD, lanes] = v[y]
                    if step < 2:
                        at = plane - 1 - step
                        store_scaled((u1f, u2f)[step], slice(at * PAD, (at + 1) * PAD), lanes, scales, v)
                    else:
                        for y in range(NY):
                            start = p * CELLS + turned(plane - 3) * NY + y
                            flat[pl.ds(start, COMP, stride=NP * CELLS), :] = v[y][0:COMP]
                    fields.append(v)
            if own:
                moments.add(step + 1, plane - 3, fields)

    lane = lax.broadcasted_iota(jnp.int32, (4, NZ), 1)
    total = jnp.zeros((4, NZ), jnp.float32)
    for j in range(WIN):
        stacked = jnp.concatenate([jnp.sum(moments.sums[n, j], axis=0, keepdims=True) for n in range(4)], axis=0)
        value = jnp.sum(stacked, axis=1, keepdims=True)
        total = total + jnp.where(lane == ((window_of(own_index()) + j) & 127), value, 0.0)
    pm_ref[...] = jnp.broadcast_to(total[None], pm_ref.shape)


HBM = pl.BlockSpec(memory_space=pltpu.HBM)
VMEM = pl.BlockSpec(memory_space=pltpu.VMEM)
SMEM = pl.BlockSpec(memory_space=pltpu.SMEM)


def body(site_class, probe_signs, masses, force_blocks):
    payload = pl.pallas_call(
        payload_kernel,
        out_shape=pltpu.VMEM((PAY_PAD, NZ), jnp.int32),
        in_specs=[HBM, HBM],
        out_specs=VMEM,
        scratch_shapes=[pltpu.SemaphoreType.DMA((2,))],
        cost_estimate=pl.CostEstimate(flops=0, bytes_accessed=800000, transcendentals=0),
        name="payload",
    )(probe_signs.reshape(COMP * NP * CX, NY, NZ), site_class.reshape(ATOMS * CX, NY, NZ))

    count = 64
    far = lax.ppermute(payload, SPACE, [(i, (i + 1) % count if i % 2 else (i - 1) % count) for i in range(count)])
    slab = HALF + (BAND, WIDE)
    *prepared, again = pl.pallas_call(
        prepare_kernel,
        out_shape=(
            pltpu.VMEM((2, 2 * BAND, 2 * BAND), jnp.bfloat16),
            pltpu.VMEM((8, NZ), jnp.float32),
            pltpu.VMEM(slab, jnp.bfloat16),
            pltpu.VMEM((CX * ROWS, WIDE), jnp.float32),
            pltpu.VMEM((CX * ROWS, NZ), jnp.float32),
            pltpu.VMEM((CX * ROWS, NZ), jnp.int32),
            pltpu.VMEM((2 * PAY_PAD, NZ), jnp.int32),
        ),
        in_specs=[SMEM, VMEM, VMEM],
        out_specs=(VMEM,) * 7,
        scratch_shapes=[pltpu.VMEM((2, BAND, NZ), jnp.float32)],
        cost_estimate=pl.CostEstimate(flops=1000000, bytes_accessed=300000, transcendentals=0),
        name="prepare",
    )(masses, force_blocks, payload)
    near = lax.all_to_all(again, "core", 0, 0, tiled=True)

    shared = pl.pallas_call(
        near_kernel,
        out_shape=(
            pltpu.VMEM(HALF + (4 * PAD, WIDE), jnp.bfloat16),
            pltpu.VMEM(HALF + (2 * PAD, WIDE), jnp.bfloat16),
            pltpu.VMEM((2 * ROWS, WIDE), jnp.float32),
            pltpu.VMEM((16 * 8, NZ), jnp.float32),
        ),
        in_specs=[VMEM] * 7,
        out_specs=(VMEM,) * 4,
        scratch_shapes=[
            pltpu.VMEM(slab, jnp.bfloat16),
            pltpu.VMEM((CX * ROWS, WIDE), jnp.float32),
            pltpu.VMEM((CX * ROWS, NZ), jnp.float32),
        ],
        compiler_params=pltpu.CompilerParams(vmem_limit_bytes=24 * 2**20),
        cost_estimate=pl.CostEstimate(flops=800000000, bytes_accessed=1000000, transcendentals=0),
        name="near_part",
    )(near, *prepared)

    group = 32
    last, parts = pl.pallas_call(
        far_kernel,
        out_shape=(
            pltpu.VMEM((COMP * NP, CX, NY, NZ), jnp.float32),
            pltpu.VMEM((group, 4, NZ), jnp.float32),
        ),
        in_specs=[VMEM] * 11,
        out_specs=(VMEM, VMEM),
        scratch_shapes=[
            pltpu.VMEM(slab, jnp.bfloat16),
            pltpu.VMEM((CX * ROWS, WIDE), jnp.float32),
            pltpu.VMEM((CX * ROWS, NZ), jnp.float32),
            pltpu.VMEM(slab, jnp.bfloat16),
            pltpu.VMEM(slab, jnp.bfloat16),
            pltpu.VMEM((ROWS, WIDE), jnp.float32),
        ],
        compiler_params=pltpu.CompilerParams(vmem_limit_bytes=24 * 2**20),
        cost_estimate=pl.CostEstimate(flops=1200000000, bytes_accessed=2000000, transcendentals=0),
        name="far_part",
    )(far, *prepared, *shared)

    parts = lax.all_to_all(parts, NEAR, 0, 0, tiled=True).sum(0)
    parts = jnp.broadcast_to(parts[None], (lax.axis_size("z"), 4, NZ))
    moments = lax.all_to_all(parts, "z", 0, 0, tiled=True).sum(0) * (1.0 / 368640)
    return moments, last.reshape(COMP, NP, CX, NY, NZ)


def solution(mesh):
    fine = Mesh(mesh.devices.reshape(2, 16, 2, 2, 4), SPACE + PROBE)
    return jax.shard_map(
        body,
        mesh=fine,
        in_specs=(P(None, SPACE, None, None), P(None, PROBE, SPACE, None, None), P(), P()),
        out_specs=(P(), P(None, PROBE, SPACE, None, None)),
        check_vma=False,
    )
```

```python
import jax
import jax.numpy as jnp
from jax import lax
from jax.experimental import pallas as pl
from jax.experimental.pallas import tpu as pltpu
from jax.sharding import Mesh, PartitionSpec as P

SPACE = ("xl", "z", "core")
PROBE = ("xh", "y")
NEAR = ("xl", "core", "xh", "y")

COMP, PAD = 30, 32
ATOMS, ATOM_PAD = 10, 16
NP, CX, NY, NZ = 4, 3, 2, 128
CELLS = CX * NY
ROWS = NY * PAD
WIDE = NP * NZ
SIGN_ROWS = COMP * NP * CELLS
LABEL_ROWS = ATOMS * CELLS
PAY_ROWS = SIGN_ROWS + LABEL_ROWS
PAY_PAD = PAY_ROWS + 4
WIN = 4
BAND = 3 * PAD
HALF = (2, 2)


def split(u):
    hi = u.astype(jnp.bfloat16)
    return hi, (u - hi.astype(jnp.float32)).astype(jnp.bfloat16)


def window_of(idx):
    return 2 * (idx & 63)


def own_index():
    return (lax.axis_index("xl") * lax.axis_size("z") + lax.axis_index("z")) * 2 + lax.axis_index("core")


def turned(k):
    return jnp.where(lax.axis_index("core") == 0, k, 2 - k)


def neighbour(slab):
    return own_index() + jnp.where(lax.axis_index("core") == 0, slab - 1, 1 - slab)


def store_scaled(u_ref, at, lanes, scales, fields):
    first, second = scales[0] * fields[0], scales[1] * fields[1]
    for sign, u in enumerate((first + second, first - second)):
        u_ref[sign, 0, at, lanes], u_ref[sign, 1, at, lanes] = split(u)


def load_slab(pay_ref, base, inv, u_ref, v0_ref, s_ref, rel_ref=None, offset=0):
    spread = (
        lax.broadcasted_iota(jnp.int32, (PAD, ATOM_PAD), 0) // 3
        == lax.broadcasted_iota(jnp.int32, (PAD, ATOM_PAD), 1)
    ).astype(jnp.bfloat16)
    valid = lax.broadcasted_iota(jnp.int32, (PAD, NZ), 0) < COMP
    cell = [turned(i // NY) * NY + i % NY for i in range(CELLS)]
    labels = jnp.concatenate(
        [pay_ref[pl.ds(offset + SIGN_ROWS + cell[i], ATOMS, stride=CELLS), :] for i in range(CELLS)], axis=1
    )
    labels = jnp.concatenate([labels, jnp.zeros((ATOM_PAD - ATOMS, CELLS * NZ), jnp.int32)], axis=0)
    labels = jnp.dot(spread, labels.astype(jnp.float32).astype(jnp.bfloat16), preferred_element_type=jnp.float32)
    rel = (labels.astype(jnp.int32) - base) & 127
    for x in range(CX):
        scales = []
        for y in range(NY):
            i = x * NY + y
            part = rel[:, i * NZ : (i + 1) * NZ]
            scale = jnp.where(part == 0, inv[0], jnp.where(part == 1, inv[1], jnp.where(part == 2, inv[2], inv[3])))
            scales.append(jnp.where(valid, scale, 0.0))
            at = slice(i * PAD, (i + 1) * PAD)
            s_ref[at, :] = scales[y]
            if rel_ref is not None:
                rel_ref[at, :] = jnp.where(valid, part, -1)
        for p in range(NP):
            lanes = slice(p * NZ, (p + 1) * NZ)
            fields = []
            for y in range(NY):
                i = x * NY + y
                sign = pay_ref[pl.ds(offset + p * CELLS + cell[i], COMP, stride=NP * CELLS), :]
                sign = jnp.concatenate([sign, jnp.zeros((PAD - COMP, NZ), jnp.int32)], axis=0)
                fields.append((2 * sign - 1).astype(jnp.float32))
                v0_ref[i * PAD : (i + 1) * PAD, lanes] = fields[y]
            store_scaled(u_ref, slice(x * PAD, (x + 1) * PAD), lanes, scales, fields)


def stencil(w_ref, planes, pair):
    lanes = slice(pair * 2 * NZ, (pair + 1) * 2 * NZ)
    sums = []
    for sign in range(2):
        field = jnp.concatenate(
            [ref[sign, part, at * PAD : (at + 1) * PAD, lanes] for part in range(2) for ref, at in planes], axis=0
        )
        t = jnp.dot(w_ref[sign], field, preferred_element_type=jnp.float32)
        o = t[0:BAND] + t[BAND:]
        sums.append(
            [
                pltpu.roll(o[0:PAD, c], 1, 1) + o[PAD : 2 * PAD, c] + pltpu.roll(o[2 * PAD :, c], NZ - 1, 1)
                for c in (slice(0, NZ), slice(NZ, 2 * NZ))
            ]
        )
    even, odd = sums
    return [(even[q] + odd[q], even[q] - odd[q]) for q in range(2)]


def cell_rows(ref, plane, lanes):
    return [ref[(plane * NY + y) * PAD : (plane * NY + y + 1) * PAD, lanes] for y in range(NY)]


ALL = slice(None)


class Moments:
    def __init__(self, rel_ref, v0_ref):
        self.rel_ref, self.v0_ref, self.sums = rel_ref, v0_ref, {}

    def add(self, n, x, fields):
        rels = cell_rows(self.rel_ref, x, ALL)
        for y in range(NY):
            total = 0.0
            for p, field in fields.items():
                total = total + cell_rows(self.v0_ref, x, slice(p * NZ, (p + 1) * NZ))[y] * field[y]
            for j in range(WIN):
                picked = jnp.where(rels[y] == j, total, 0.0)
                part = sum(picked[8 * k : 8 * k + 8] for k in range(PAD // 8))
                self.sums[n, j] = self.sums[n, j] + part if (n, j) in self.sums else part


def payload_kernel(signs_ref, labels_ref, pay_ref, sems):
    copies = [
        pltpu.make_async_copy(signs_ref.reshape(SIGN_ROWS, NZ), pay_ref.at[0:SIGN_ROWS, :], sems.at[0]),
        pltpu.make_async_copy(labels_ref.reshape(LABEL_ROWS, NZ), pay_ref.at[SIGN_ROWS:PAY_ROWS, :], sems.at[1]),
    ]
    for copy in copies:
        copy.start()
    for copy in copies:
        copy.wait()


def prepare_kernel(mass_ref, fb_ref, own_ref, w_ref, inv_ref, u_ref, v0_ref, s_ref, rel_ref, again_ref, full):
    for k in range(2):
        again_ref[k * PAY_PAD : (k + 1) * PAY_PAD, :] = own_ref[...]
    full[...] = jnp.zeros_like(full)
    for k in range(3):
        dx = turned(k)
        for dz in range(3):
            same = fb_ref[9 * dx + 3 + dz]
            other = fb_ref[9 * dx + dz] + fb_ref[9 * dx + 6 + dz]
            r, c = dz * PAD, k * PAD
            full[0, r : r + COMP, c : c + COMP] = 0.5 * (same + other)
            full[1, r : r + COMP, c : c + COMP] = 0.5 * (same - other)
    for sign in range(2):
        hi, lo = split(full[sign])
        w_ref[sign, 0:BAND, :] = jnp.concatenate([hi[:, 0:BAND], hi[:, 0:BAND]], axis=1)
        w_ref[sign, BAND:, :] = jnp.concatenate([lo[:, 0:BAND], jnp.zeros((BAND, BAND), jnp.bfloat16)], axis=1)

    for slab in range(3):
        base = window_of(neighbour(slab))
        inv = [1.0 / jnp.sqrt(jnp.full((1, NZ), mass_ref[(base + j) & 127], jnp.float32)) for j in range(WIN)]
        if slab == 1:
            load_slab(own_ref, base, inv, u_ref, v0_ref, s_ref, rel_ref)
        else:
            for j in range(WIN):
                at = slab * 2 + j
                inv_ref[at : at + 1, :] = inv[j]


def near_kernel(pay_ref, w_ref, inv_ref, u0, v0, s, rel, u1_ref, u2_ref, v1_ref, sums_ref, u0n, v0n, sn):
    inv = [inv_ref[4 + j : 5 + j, :] for j in range(WIN)]
    offset = (1 - lax.axis_index("core")) * PAY_PAD
    load_slab(pay_ref, window_of(neighbour(2)), inv, u0n, v0n, sn, offset=offset)
    moments = Moments(rel, v0)
    lanes_of = [slice(p * NZ, (p + 1) * NZ) for p in range(NP)]
    for x in range(CX):
        moments.add(0, x, {p: cell_rows(v0, x, lanes_of[p]) for p in range(NP)})

    def first(plane):
        return (u0, plane - 3) if plane < 6 else (u0n, plane - 6)

    def scales_of(plane):
        return cell_rows(s, plane - 3, ALL) if plane < 6 else cell_rows(sn, plane - 6, ALL)

    for pair in range(NP // 2):
        for plane in (4, 5, 6, 7):
            scales, fields = scales_of(plane), {}
            for q, g in enumerate(stencil(w_ref, [first(plane + d) for d in (-1, 0, 1)], pair)):
                p = 2 * pair + q
                lanes = lanes_of[p]
                v = fields[p] = [scales[y] * g[y] for y in range(NY)]
                store_scaled(u1_ref, slice((plane - 4) * PAD, (plane - 3) * PAD), lanes, scales, v)
                if plane < 6:
                    for y in range(NY):
                        at = (plane - 4) * ROWS + y * PAD
                        v1_ref[at : at + PAD, lanes] = v[y]
            if plane < 6:
                moments.add(1, plane - 3, fields)
    for pair in range(NP // 2):
        for plane in (5, 6):
            scales, fields = scales_of(plane), {}
            for q, g in enumerate(stencil(w_ref, [(u1_ref, plane - 4 + d) for d in (-1, 0, 1)], pair)):
                p = 2 * pair + q
                lanes = lanes_of[p]
                before = cell_rows(v0, 2, lanes) if plane == 5 else cell_rows(v0n, 0, lanes)
                v = fields[p] = [2.0 * (scales[y] * g[y]) - before[y] for y in range(NY)]
                store_scaled(u2_ref, slice((plane - 5) * PAD, (plane - 4) * PAD), lanes, scales, v)
            if plane == 5:
                moments.add(2, 2, fields)
    for n in range(4):
        for j in range(WIN):
            at = (n * WIN + j) * 8
            sums_ref[at : at + 8, :] = moments.sums.get((n, j), jnp.zeros((8, NZ), jnp.float32))


def far_kernel(
    pay_ref, w_ref, inv_ref, u0, v0, s, rel, u1, u2, v1, sums_ref, out_ref, pm_ref, u0f, v0f, sf, u1f, u2f, v1f
):
    inv = [inv_ref[j : j + 1, :] for j in range(WIN)]
    load_slab(pay_ref, window_of(neighbour(0)), inv, u0f, v0f, sf)
    moments = Moments(rel, v0)
    for n in range(4):
        for j in range(WIN):
            at = (n * WIN + j) * 8
            moments.sums[n, j] = sums_ref[at : at + 8, :]
    lanes_of = [slice(p * NZ, (p + 1) * NZ) for p in range(NP)]

    def source(step, plane):
        if step == 0:
            return (u0f, plane) if plane < 3 else (u0, plane - 3)
        if step == 1:
            return (u1f, plane - 1) if plane < 4 else (u1, plane - 4)
        return (u2f, plane - 2) if plane < 5 else (u2, plane - 5)

    flat = out_ref.reshape(SIGN_ROWS, NZ)
    for step in range(3):
        for pair, plane in [(pair, plane) for pair in range(NP // 2) for plane in range(step + 1, step + 4)]:
            own = plane >= 3
            scales = cell_rows(s, plane - 3, ALL) if own else cell_rows(sf, plane, ALL)
            fields = {}
            planes = [source(step, plane + d) for d in (-1, 0, 1)]
            for q, g in enumerate(stencil(w_ref, planes, pair)):
                p = 2 * pair + q
                lanes = lanes_of[p]
                v = [scales[y] * g[y] for y in range(NY)]
                if step == 1:
                    before = cell_rows(v0, plane - 3, lanes) if own else cell_rows(v0f, plane, lanes)
                    v = [2.0 * v[y] - before[y] for y in range(NY)]
                elif step == 2:
                    before = cell_rows(v1f, 0, lanes) if plane == 3 else cell_rows(v1, plane - 4, lanes)
                    v = [2.0 * v[y] - before[y] for y in range(NY)]
                fields[p] = v
                if step == 0 and own:
                    for y in range(NY):
                        v1f[y * PAD : (y + 1) * PAD, lanes] = v[y]
                if step < 2:
                    at = plane - 1 - step
                    store_scaled((u1f, u2f)[step], slice(at * PAD, (at + 1) * PAD), lanes, scales, v)
                else:
                    for y in range(NY):
                        start = p * CELLS + turned(plane - 3) * NY + y
                        flat[pl.ds(start, COMP, stride=NP * CELLS), :] = v[y][0:COMP]
            if own:
                moments.add(step + 1, plane - 3, fields)

    lane = lax.broadcasted_iota(jnp.int32, (4, NZ), 1)
    total = jnp.zeros((4, NZ), jnp.float32)
    for j in range(WIN):
        stacked = jnp.concatenate([jnp.sum(moments.sums[n, j], axis=0, keepdims=True) for n in range(4)], axis=0)
        value = jnp.sum(stacked, axis=1, keepdims=True)
        total = total + jnp.where(lane == ((window_of(own_index()) + j) & 127), value, 0.0)
    pm_ref[...] = jnp.broadcast_to(total[None], pm_ref.shape)


HBM = pl.BlockSpec(memory_space=pltpu.HBM)
VMEM = pl.BlockSpec(memory_space=pltpu.VMEM)
SMEM = pl.BlockSpec(memory_space=pltpu.SMEM)


def body(site_class, probe_signs, masses, force_blocks):
    payload = pl.pallas_call(
        payload_kernel,
        out_shape=pltpu.VMEM((PAY_PAD, NZ), jnp.int32),
        in_specs=[HBM, HBM],
        out_specs=VMEM,
        scratch_shapes=[pltpu.SemaphoreType.DMA((2,))],
        cost_estimate=pl.CostEstimate(flops=0, bytes_accessed=800000, transcendentals=0),
        name="payload",
    )(probe_signs.reshape(COMP * NP * CX, NY, NZ), site_class.reshape(ATOMS * CX, NY, NZ))

    count = 64
    far = lax.ppermute(payload, SPACE, [(i, (i + 1) % count if i % 2 else (i - 1) % count) for i in range(count)])
    slab = HALF + (BAND, WIDE)
    *prepared, again = pl.pallas_call(
        prepare_kernel,
        out_shape=(
            pltpu.VMEM((2, 2 * BAND, 2 * BAND), jnp.bfloat16),
            pltpu.VMEM((8, NZ), jnp.float32),
            pltpu.VMEM(slab, jnp.bfloat16),
            pltpu.VMEM((CX * ROWS, WIDE), jnp.float32),
            pltpu.VMEM((CX * ROWS, NZ), jnp.float32),
            pltpu.VMEM((CX * ROWS, NZ), jnp.int32),
            pltpu.VMEM((2 * PAY_PAD, NZ), jnp.int32),
        ),
        in_specs=[SMEM, VMEM, VMEM],
        out_specs=(VMEM,) * 7,
        scratch_shapes=[pltpu.VMEM((2, BAND, NZ), jnp.float32)],
        cost_estimate=pl.CostEstimate(flops=1000000, bytes_accessed=300000, transcendentals=0),
        name="prepare",
    )(masses, force_blocks, payload)
    near = lax.all_to_all(again, "core", 0, 0, tiled=True)

    shared = pl.pallas_call(
        near_kernel,
        out_shape=(
            pltpu.VMEM(HALF + (4 * PAD, WIDE), jnp.bfloat16),
            pltpu.VMEM(HALF + (2 * PAD, WIDE), jnp.bfloat16),
            pltpu.VMEM((2 * ROWS, WIDE), jnp.float32),
            pltpu.VMEM((16 * 8, NZ), jnp.float32),
        ),
        in_specs=[VMEM] * 7,
        out_specs=(VMEM,) * 4,
        scratch_shapes=[
            pltpu.VMEM(slab, jnp.bfloat16),
            pltpu.VMEM((CX * ROWS, WIDE), jnp.float32),
            pltpu.VMEM((CX * ROWS, NZ), jnp.float32),
        ],
        compiler_params=pltpu.CompilerParams(vmem_limit_bytes=24 * 2**20),
        cost_estimate=pl.CostEstimate(flops=800000000, bytes_accessed=1000000, transcendentals=0),
        name="near_part",
    )(near, *prepared)

    group = 32
    last, parts = pl.pallas_call(
        far_kernel,
        out_shape=(
            pltpu.VMEM((COMP * NP, CX, NY, NZ), jnp.float32),
            pltpu.VMEM((group, 4, NZ), jnp.float32),
        ),
        in_specs=[VMEM] * 11,
        out_specs=(VMEM, VMEM),
        scratch_shapes=[
            pltpu.VMEM(slab, jnp.bfloat16),
            pltpu.VMEM((CX * ROWS, WIDE), jnp.float32),
            pltpu.VMEM((CX * ROWS, NZ), jnp.float32),
            pltpu.VMEM(slab, jnp.bfloat16),
            pltpu.VMEM(slab, jnp.bfloat16),
            pltpu.VMEM((ROWS, WIDE), jnp.float32),
        ],
        compiler_params=pltpu.CompilerParams(vmem_limit_bytes=24 * 2**20),
        cost_estimate=pl.CostEstimate(flops=1200000000, bytes_accessed=2000000, transcendentals=0),
        name="far_part",
    )(far, *prepared, *shared)

    parts = lax.all_to_all(parts, NEAR, 0, 0, tiled=True).sum(0)
    parts = jnp.broadcast_to(parts[None], (lax.axis_size("z"), 4, NZ))
    moments = lax.all_to_all(parts, "z", 0, 0, tiled=True).sum(0) * (1.0 / 368640)
    return moments, last.reshape(COMP, NP, CX, NY, NZ)


def solution(mesh):
    fine = Mesh(mesh.devices.reshape(2, 16, 2, 2, 4), SPACE + PROBE)
    return jax.shard_map(
        body,
        mesh=fine,
        in_specs=(P(None, SPACE, None, None), P(None, PROBE, SPACE, None, None), P(), P()),
        out_specs=(P(), P(None, PROBE, SPACE, None, None)),
        check_vma=False,
    )
```

```python
import jax
import jax.numpy as jnp
from jax import lax
from jax.experimental import pallas as pl
from jax.experimental.pallas import tpu as pltpu
from jax.sharding import Mesh, PartitionSpec as P

SPACE = ("xl", "z", "core")
PROBE = ("xh", "y")
NEAR = ("xl", "core", "xh", "y")

COMP, PAD = 30, 32
ATOMS, ATOM_PAD = 10, 16
NP, CX, NY, NZ = 4, 3, 2, 128
CELLS = CX * NY
ROWS = NY * PAD
WIDE = NP * NZ
SIGN_ROWS = COMP * NP * CELLS
LABEL_ROWS = ATOMS * CELLS
PAY_ROWS = SIGN_ROWS + LABEL_ROWS
PAY_PAD = PAY_ROWS + 4
WIN = 4
BAND = 3 * PAD
HALF = (2, 2)


def split(u):
    hi = u.astype(jnp.bfloat16)
    return hi, (u - hi.astype(jnp.float32)).astype(jnp.bfloat16)


def window_of(idx):
    return 2 * (idx & 63)


def own_index():
    return (lax.axis_index("xl") * lax.axis_size("z") + lax.axis_index("z")) * 2 + lax.axis_index("core")


def turned(k):
    return jnp.where(lax.axis_index("core") == 0, k, 2 - k)


def neighbour(slab):
    return own_index() + jnp.where(lax.axis_index("core") == 0, slab - 1, 1 - slab)


def store_scaled(u_ref, at, lanes, scales, fields):
    first, second = scales[0] * fields[0], scales[1] * fields[1]
    for sign, u in enumerate((first + second, first - second)):
        u_ref[sign, 0, at, lanes], u_ref[sign, 1, at, lanes] = split(u)


def load_slab(pay_ref, base, inv, u_ref, v0_ref, s_ref, rel_ref=None, offset=0):
    spread = (
        lax.broadcasted_iota(jnp.int32, (PAD, ATOM_PAD), 0) // 3
        == lax.broadcasted_iota(jnp.int32, (PAD, ATOM_PAD), 1)
    ).astype(jnp.bfloat16)
    valid = lax.broadcasted_iota(jnp.int32, (PAD, NZ), 0) < COMP
    cell = [turned(i // NY) * NY + i % NY for i in range(CELLS)]
    labels = jnp.concatenate(
        [pay_ref[pl.ds(offset + SIGN_ROWS + cell[i], ATOMS, stride=CELLS), :] for i in range(CELLS)], axis=1
    )
    labels = jnp.concatenate([labels, jnp.zeros((ATOM_PAD - ATOMS, CELLS * NZ), jnp.int32)], axis=0)
    labels = jnp.dot(spread, labels.astype(jnp.float32).astype(jnp.bfloat16), preferred_element_type=jnp.float32)
    rel = (labels.astype(jnp.int32) - base) & 127
    for x in range(CX):
        scales = []
        for y in range(NY):
            i = x * NY + y
            part = rel[:, i * NZ : (i + 1) * NZ]
            scale = jnp.where(part == 0, inv[0], jnp.where(part == 1, inv[1], jnp.where(part == 2, inv[2], inv[3])))
            scales.append(jnp.where(valid, scale, 0.0))
            at = slice(i * PAD, (i + 1) * PAD)
            s_ref[at, :] = scales[y]
            if rel_ref is not None:
                rel_ref[at, :] = jnp.where(valid, part, -1)
        for p in range(NP):
            lanes = slice(p * NZ, (p + 1) * NZ)
            fields = []
            for y in range(NY):
                i = x * NY + y
                sign = pay_ref[pl.ds(offset + p * CELLS + cell[i], COMP, stride=NP * CELLS), :]
                sign = jnp.concatenate([sign, jnp.zeros((PAD - COMP, NZ), jnp.int32)], axis=0)
                fields.append((2 * sign - 1).astype(jnp.float32))
                v0_ref[i * PAD : (i + 1) * PAD, lanes] = fields[y]
            store_scaled(u_ref, slice(x * PAD, (x + 1) * PAD), lanes, scales, fields)


def stencil(w_ref, planes, pair):
    lanes = slice(pair * 2 * NZ, (pair + 1) * 2 * NZ)
    sums = []
    for sign in range(2):
        field = jnp.concatenate(
            [ref[sign, part, at * PAD : (at + 1) * PAD, lanes] for part in range(2) for ref, at in planes], axis=0
        )
        t = jnp.dot(w_ref[sign], field, preferred_element_type=jnp.float32)
        o = t[0:BAND] + t[BAND:]
        sums.append(
            [
                pltpu.roll(o[0:PAD, c], 1, 1) + o[PAD : 2 * PAD, c] + pltpu.roll(o[2 * PAD :, c], NZ - 1, 1)
                for c in (slice(0, NZ), slice(NZ, 2 * NZ))
            ]
        )
    even, odd = sums
    return [(even[q] + odd[q], even[q] - odd[q]) for q in range(2)]


def cell_rows(ref, plane, lanes):
    return [ref[(plane * NY + y) * PAD : (plane * NY + y + 1) * PAD, lanes] for y in range(NY)]


ALL = slice(None)


class Moments:
    def __init__(self, rel_ref, v0_ref):
        self.rel_ref, self.v0_ref, self.sums = rel_ref, v0_ref, {}

    def add(self, n, x, fields):
        rels = cell_rows(self.rel_ref, x, ALL)
        for y in range(NY):
            total = 0.0
            for p, field in fields.items():
                total = total + cell_rows(self.v0_ref, x, slice(p * NZ, (p + 1) * NZ))[y] * field[y]
            for j in range(WIN):
                picked = jnp.where(rels[y] == j, total, 0.0)
                part = sum(picked[8 * k : 8 * k + 8] for k in range(PAD // 8))
                self.sums[n, j] = self.sums[n, j] + part if (n, j) in self.sums else part


def payload_kernel(signs_ref, labels_ref, pay_ref, sems):
    copies = [
        pltpu.make_async_copy(signs_ref.reshape(SIGN_ROWS, NZ), pay_ref.at[0:SIGN_ROWS, :], sems.at[0]),
        pltpu.make_async_copy(labels_ref.reshape(LABEL_ROWS, NZ), pay_ref.at[SIGN_ROWS:PAY_ROWS, :], sems.at[1]),
    ]
    for copy in copies:
        copy.start()
    for copy in copies:
        copy.wait()


def prepare_kernel(mass_ref, fb_ref, own_ref, w_ref, inv_ref, u_ref, v0_ref, s_ref, rel_ref, again_ref, full):
    for k in range(2):
        again_ref[k * PAY_PAD : (k + 1) * PAY_PAD, :] = own_ref[...]
    full[...] = jnp.zeros_like(full)
    for k in range(3):
        dx = turned(k)
        for dz in range(3):
            same = fb_ref[9 * dx + 3 + dz]
            other = fb_ref[9 * dx + dz] + fb_ref[9 * dx + 6 + dz]
            r, c = dz * PAD, k * PAD
            full[0, r : r + COMP, c : c + COMP] = 0.5 * (same + other)
            full[1, r : r + COMP, c : c + COMP] = 0.5 * (same - other)
    for sign in range(2):
        hi, lo = split(full[sign])
        w_ref[sign, 0:BAND, :] = jnp.concatenate([hi[:, 0:BAND], hi[:, 0:BAND]], axis=1)
        w_ref[sign, BAND:, :] = jnp.concatenate([lo[:, 0:BAND], jnp.zeros((BAND, BAND), jnp.bfloat16)], axis=1)

    for slab in range(3):
        base = window_of(neighbour(slab))
        inv = [1.0 / jnp.sqrt(jnp.full((1, NZ), mass_ref[(base + j) & 127], jnp.float32)) for j in range(WIN)]
        if slab == 1:
            load_slab(own_ref, base, inv, u_ref, v0_ref, s_ref, rel_ref)
        else:
            for j in range(WIN):
                at = slab * 2 + j
                inv_ref[at : at + 1, :] = inv[j]


def near_kernel(pay_ref, w_ref, inv_ref, u0, v0, s, rel, u1_ref, u2_ref, v1_ref, sums_ref, u0n, v0n, sn):
    inv = [inv_ref[4 + j : 5 + j, :] for j in range(WIN)]
    offset = (1 - lax.axis_index("core")) * PAY_PAD
    load_slab(pay_ref, window_of(neighbour(2)), inv, u0n, v0n, sn, offset=offset)
    moments = Moments(rel, v0)
    lanes_of = [slice(p * NZ, (p + 1) * NZ) for p in range(NP)]
    for x in range(CX):
        moments.add(0, x, {p: cell_rows(v0, x, lanes_of[p]) for p in range(NP)})

    def first(plane):
        return (u0, plane - 3) if plane < 6 else (u0n, plane - 6)

    def scales_of(plane):
        return cell_rows(s, plane - 3, ALL) if plane < 6 else cell_rows(sn, plane - 6, ALL)

    for pair in range(NP // 2):
        for plane in (4, 5, 6, 7):
            scales, fields = scales_of(plane), {}
            for q, g in enumerate(stencil(w_ref, [first(plane + d) for d in (-1, 0, 1)], pair)):
                p = 2 * pair + q
                lanes = lanes_of[p]
                v = fields[p] = [scales[y] * g[y] for y in range(NY)]
                store_scaled(u1_ref, slice((plane - 4) * PAD, (plane - 3) * PAD), lanes, scales, v)
                if plane < 6:
                    for y in range(NY):
                        at = (plane - 4) * ROWS + y * PAD
                        v1_ref[at : at + PAD, lanes] = v[y]
            if plane < 6:
                moments.add(1, plane - 3, fields)
    for pair in range(NP // 2):
        for plane in (5, 6):
            scales, fields = scales_of(plane), {}
            for q, g in enumerate(stencil(w_ref, [(u1_ref, plane - 4 + d) for d in (-1, 0, 1)], pair)):
                p = 2 * pair + q
                lanes = lanes_of[p]
                before = cell_rows(v0, 2, lanes) if plane == 5 else cell_rows(v0n, 0, lanes)
                v = fields[p] = [2.0 * (scales[y] * g[y]) - before[y] for y in range(NY)]
                store_scaled(u2_ref, slice((plane - 5) * PAD, (plane - 4) * PAD), lanes, scales, v)
            if plane == 5:
                moments.add(2, 2, fields)
    for n in range(4):
        for j in range(WIN):
            at = (n * WIN + j) * 8
            sums_ref[at : at + 8, :] = moments.sums.get((n, j), jnp.zeros((8, NZ), jnp.float32))


def far_kernel(
    pay_ref, w_ref, inv_ref, u0, v0, s, rel, u1, u2, v1, sums_ref, out_ref, pm_ref, u0f, v0f, sf, u1f, u2f, v1f
):
    inv = [inv_ref[j : j + 1, :] for j in range(WIN)]
    load_slab(pay_ref, window_of(neighbour(0)), inv, u0f, v0f, sf)
    moments = Moments(rel, v0)
    for n in range(4):
        for j in range(WIN):
            at = (n * WIN + j) * 8
            moments.sums[n, j] = sums_ref[at : at + 8, :]
    lanes_of = [slice(p * NZ, (p + 1) * NZ) for p in range(NP)]

    def source(step, plane):
        if step == 0:
            return (u0f, plane) if plane < 3 else (u0, plane - 3)
        if step == 1:
            return (u1f, plane - 1) if plane < 4 else (u1, plane - 4)
        return (u2f, plane - 2) if plane < 5 else (u2, plane - 5)

    flat = out_ref.reshape(SIGN_ROWS, NZ)
    for step in range(3):
        for pair, plane in [(pair, plane) for pair in range(NP // 2) for plane in range(step + 1, step + 4)]:
            own = plane >= 3
            scales = cell_rows(s, plane - 3, ALL) if own else cell_rows(sf, plane, ALL)
            fields = {}
            planes = [source(step, plane + d) for d in (-1, 0, 1)]
            for q, g in enumerate(stencil(w_ref, planes, pair)):
                p = 2 * pair + q
                lanes = lanes_of[p]
                v = [scales[y] * g[y] for y in range(NY)]
                if step == 1:
                    before = cell_rows(v0, plane - 3, lanes) if own else cell_rows(v0f, plane, lanes)
                    v = [2.0 * v[y] - before[y] for y in range(NY)]
                elif step == 2:
                    before = cell_rows(v1f, 0, lanes) if plane == 3 else cell_rows(v1, plane - 4, lanes)
                    v = [2.0 * v[y] - before[y] for y in range(NY)]
                fields[p] = v
                if step == 0 and own:
                    for y in range(NY):
                        v1f[y * PAD : (y + 1) * PAD, lanes] = v[y]
                if step < 2:
                    at = plane - 1 - step
                    store_scaled((u1f, u2f)[step], slice(at * PAD, (at + 1) * PAD), lanes, scales, v)
                else:
                    for y in range(NY):
                        start = p * CELLS + turned(plane - 3) * NY + y
                        flat[pl.ds(start, COMP, stride=NP * CELLS), :] = v[y][0:COMP]
            if own:
                moments.add(step + 1, plane - 3, fields)

    lane = lax.broadcasted_iota(jnp.int32, (4, NZ), 1)
    total = jnp.zeros((4, NZ), jnp.float32)
    for j in range(WIN):
        stacked = jnp.concatenate([jnp.sum(moments.sums[n, j], axis=0, keepdims=True) for n in range(4)], axis=0)
        value = jnp.sum(stacked, axis=1, keepdims=True)
        total = total + jnp.where(lane == ((window_of(own_index()) + j) & 127), value, 0.0)
    pm_ref[...] = jnp.broadcast_to(total[None], pm_ref.shape)


HBM = pl.BlockSpec(memory_space=pltpu.HBM)
VMEM = pl.BlockSpec(memory_space=pltpu.VMEM)
SMEM = pl.BlockSpec(memory_space=pltpu.SMEM)


def body(site_class, probe_signs, masses, force_blocks):
    payload = pl.pallas_call(
        payload_kernel,
        out_shape=pltpu.VMEM((PAY_PAD, NZ), jnp.int32),
        in_specs=[HBM, HBM],
        out_specs=VMEM,
        scratch_shapes=[pltpu.SemaphoreType.DMA((2,))],
        cost_estimate=pl.CostEstimate(flops=0, bytes_accessed=800000, transcendentals=0),
        name="payload",
    )(probe_signs.reshape(COMP * NP * CX, NY, NZ), site_class.reshape(ATOMS * CX, NY, NZ))

    count = 64
    far = lax.ppermute(payload, SPACE, [(i, (i + 1) % count if i % 2 else (i - 1) % count) for i in range(count)])
    slab = HALF + (BAND, WIDE)
    *prepared, again = pl.pallas_call(
        prepare_kernel,
        out_shape=(
            pltpu.VMEM((2, 2 * BAND, 2 * BAND), jnp.bfloat16),
            pltpu.VMEM((8, NZ), jnp.float32),
            pltpu.VMEM(slab, jnp.bfloat16),
            pltpu.VMEM((CX * ROWS, WIDE), jnp.float32),
            pltpu.VMEM((CX * ROWS, NZ), jnp.float32),
            pltpu.VMEM((CX * ROWS, NZ), jnp.int32),
            pltpu.VMEM((2 * PAY_PAD, NZ), jnp.int32),
        ),
        in_specs=[SMEM, VMEM, VMEM],
        out_specs=(VMEM,) * 7,
        scratch_shapes=[pltpu.VMEM((2, BAND, NZ), jnp.float32)],
        cost_estimate=pl.CostEstimate(flops=1000000, bytes_accessed=300000, transcendentals=0),
        name="prepare",
    )(masses, force_blocks, payload)
    near = lax.all_to_all(again, "core", 0, 0, tiled=True)

    shared = pl.pallas_call(
        near_kernel,
        out_shape=(
            pltpu.VMEM(HALF + (4 * PAD, WIDE), jnp.bfloat16),
            pltpu.VMEM(HALF + (2 * PAD, WIDE), jnp.bfloat16),
            pltpu.VMEM((2 * ROWS, WIDE), jnp.float32),
            pltpu.VMEM((16 * 8, NZ), jnp.float32),
        ),
        in_specs=[VMEM] * 7,
        out_specs=(VMEM,) * 4,
        scratch_shapes=[
            pltpu.VMEM(slab, jnp.bfloat16),
            pltpu.VMEM((CX * ROWS, WIDE), jnp.float32),
            pltpu.VMEM((CX * ROWS, NZ), jnp.float32),
        ],
        compiler_params=pltpu.CompilerParams(vmem_limit_bytes=24 * 2**20),
        cost_estimate=pl.CostEstimate(flops=800000000, bytes_accessed=1000000, transcendentals=0),
        name="near_part",
    )(near, *prepared)

    group = lax.axis_size("z")
    last, parts = pl.pallas_call(
        far_kernel,
        out_shape=(
            pltpu.VMEM((COMP * NP, CX, NY, NZ), jnp.float32),
            pltpu.VMEM((group, 4, NZ), jnp.float32),
        ),
        in_specs=[VMEM] * 11,
        out_specs=(VMEM, VMEM),
        scratch_shapes=[
            pltpu.VMEM(slab, jnp.bfloat16),
            pltpu.VMEM((CX * ROWS, WIDE), jnp.float32),
            pltpu.VMEM((CX * ROWS, NZ), jnp.float32),
            pltpu.VMEM(slab, jnp.bfloat16),
            pltpu.VMEM(slab, jnp.bfloat16),
            pltpu.VMEM((ROWS, WIDE), jnp.float32),
        ],
        compiler_params=pltpu.CompilerParams(vmem_limit_bytes=24 * 2**20),
        cost_estimate=pl.CostEstimate(flops=1200000000, bytes_accessed=2000000, transcendentals=0),
        name="far_part",
    )(far, *prepared, *shared)

    parts = lax.all_to_all(parts, "z", 0, 0, tiled=True).sum(0)
    parts = jnp.broadcast_to(parts[None], (32, 4, NZ))
    moments = lax.all_to_all(parts, NEAR, 0, 0, tiled=True).sum(0) * (1.0 / 368640)
    return moments, last.reshape(COMP, NP, CX, NY, NZ)


def solution(mesh):
    fine = Mesh(mesh.devices.reshape(2, 16, 2, 2, 4), SPACE + PROBE)
    return jax.shard_map(
        body,
        mesh=fine,
        in_specs=(P(None, SPACE, None, None), P(None, PROBE, SPACE, None, None), P(), P()),
        out_specs=(P(), P(None, PROBE, SPACE, None, None)),
        check_vma=False,
    )
```

```python
import jax
import jax.numpy as jnp
from jax import lax
from jax.experimental import pallas as pl
from jax.experimental.pallas import tpu as pltpu
from jax.sharding import Mesh, PartitionSpec as P

SPACE = ("xl", "z", "core")
PROBE = ("xh", "y")
NEAR = ("xl", "core", "xh", "y")

COMP, PAD = 30, 32
ATOMS, ATOM_PAD = 10, 16
NP, CX, NY, NZ = 4, 3, 2, 128
CELLS = CX * NY
ROWS = NY * PAD
WIDE = NP * NZ
SIGN_ROWS = COMP * NP * CELLS
LABEL_ROWS = ATOMS * CELLS
PAY_ROWS = SIGN_ROWS + LABEL_ROWS
PAY_PAD = PAY_ROWS + 4
WIN = 4
BAND = 3 * PAD
HALF = (2, 2)


def split(u):
    hi = u.astype(jnp.bfloat16)
    return hi, (u - hi.astype(jnp.float32)).astype(jnp.bfloat16)


def window_of(idx):
    return 2 * (idx & 63)


def own_index():
    return (lax.axis_index("xl") * lax.axis_size("z") + lax.axis_index("z")) * 2 + lax.axis_index("core")


def turned(k):
    return jnp.where(lax.axis_index("core") == 0, k, 2 - k)


def neighbour(slab):
    return own_index() + jnp.where(lax.axis_index("core") == 0, slab - 1, 1 - slab)


def store_scaled(u_ref, at, lanes, scales, fields):
    first, second = scales[0] * fields[0], scales[1] * fields[1]
    for sign, u in enumerate((first + second, first - second)):
        u_ref[sign, 0, at, lanes], u_ref[sign, 1, at, lanes] = split(u)


def load_slab(pay_ref, base, inv, u_ref, v0_ref, s_ref, rel_ref=None, offset=0):
    spread = (
        lax.broadcasted_iota(jnp.int32, (PAD, ATOM_PAD), 0) // 3
        == lax.broadcasted_iota(jnp.int32, (PAD, ATOM_PAD), 1)
    ).astype(jnp.bfloat16)
    valid = lax.broadcasted_iota(jnp.int32, (PAD, NZ), 0) < COMP
    cell = [turned(i // NY) * NY + i % NY for i in range(CELLS)]
    labels = jnp.concatenate(
        [pay_ref[pl.ds(offset + SIGN_ROWS + cell[i], ATOMS, stride=CELLS), :] for i in range(CELLS)], axis=1
    )
    labels = jnp.concatenate([labels, jnp.zeros((ATOM_PAD - ATOMS, CELLS * NZ), jnp.int32)], axis=0)
    labels = jnp.dot(spread, labels.astype(jnp.float32).astype(jnp.bfloat16), preferred_element_type=jnp.float32)
    rel = (labels.astype(jnp.int32) - base) & 127
    for x in range(CX):
        scales = []
        for y in range(NY):
            i = x * NY + y
            part = rel[:, i * NZ : (i + 1) * NZ]
            scale = jnp.where(part == 0, inv[0], jnp.where(part == 1, inv[1], jnp.where(part == 2, inv[2], inv[3])))
            scales.append(jnp.where(valid, scale, 0.0))
            at = slice(i * PAD, (i + 1) * PAD)
            s_ref[at, :] = scales[y]
            if rel_ref is not None:
                rel_ref[at, :] = jnp.where(valid, part, -1)
        for p in range(NP):
            lanes = slice(p * NZ, (p + 1) * NZ)
            fields = []
            for y in range(NY):
                i = x * NY + y
                sign = pay_ref[pl.ds(offset + p * CELLS + cell[i], COMP, stride=NP * CELLS), :]
                sign = jnp.concatenate([sign, jnp.zeros((PAD - COMP, NZ), jnp.int32)], axis=0)
                fields.append((2 * sign - 1).astype(jnp.float32))
                v0_ref[i * PAD : (i + 1) * PAD, lanes] = fields[y]
            store_scaled(u_ref, slice(x * PAD, (x + 1) * PAD), lanes, scales, fields)


def stencil(w_ref, planes, pair):
    lanes = slice(pair * 2 * NZ, (pair + 1) * 2 * NZ)
    sums = []
    for sign in range(2):
        field = jnp.concatenate(
            [ref[sign, part, at * PAD : (at + 1) * PAD, lanes] for part in range(2) for ref, at in planes], axis=0
        )
        t = jnp.dot(w_ref[sign], field, preferred_element_type=jnp.float32)
        o = t[0:BAND] + t[BAND:]
        sums.append(
            [
                pltpu.roll(o[0:PAD, c], 1, 1) + o[PAD : 2 * PAD, c] + pltpu.roll(o[2 * PAD :, c], NZ - 1, 1)
                for c in (slice(0, NZ), slice(NZ, 2 * NZ))
            ]
        )
    even, odd = sums
    return [(even[q] + odd[q], even[q] - odd[q]) for q in range(2)]


def cell_rows(ref, plane, lanes):
    return [ref[(plane * NY + y) * PAD : (plane * NY + y + 1) * PAD, lanes] for y in range(NY)]


ALL = slice(None)


class Moments:
    def __init__(self, rel_ref, v0_ref):
        self.rel_ref, self.v0_ref, self.sums = rel_ref, v0_ref, {}

    def add(self, n, x, fields):
        rels = cell_rows(self.rel_ref, x, ALL)
        for y in range(NY):
            total = 0.0
            for p, field in fields.items():
                total = total + cell_rows(self.v0_ref, x, slice(p * NZ, (p + 1) * NZ))[y] * field[y]
            for j in range(WIN):
                picked = jnp.where(rels[y] == j, total, 0.0)
                part = sum(picked[8 * k : 8 * k + 8] for k in range(PAD // 8))
                self.sums[n, j] = self.sums[n, j] + part if (n, j) in self.sums else part


def payload_kernel(signs_ref, labels_ref, pay_ref, sems):
    copies = [
        pltpu.make_async_copy(signs_ref.reshape(SIGN_ROWS, NZ), pay_ref.at[0:SIGN_ROWS, :], sems.at[0]),
        pltpu.make_async_copy(labels_ref.reshape(LABEL_ROWS, NZ), pay_ref.at[SIGN_ROWS:PAY_ROWS, :], sems.at[1]),
    ]
    for copy in copies:
        copy.start()
    for copy in copies:
        copy.wait()


def prepare_kernel(mass_ref, fb_ref, own_ref, w_ref, inv_ref, u_ref, v0_ref, s_ref, rel_ref, again_ref, full):
    for k in range(2):
        again_ref[k * PAY_PAD : (k + 1) * PAY_PAD, :] = own_ref[...]
    full[...] = jnp.zeros_like(full)
    for k in range(3):
        dx = turned(k)
        for dz in range(3):
            same = fb_ref[9 * dx + 3 + dz]
            other = fb_ref[9 * dx + dz] + fb_ref[9 * dx + 6 + dz]
            r, c = dz * PAD, k * PAD
            full[0, r : r + COMP, c : c + COMP] = 0.5 * (same + other)
            full[1, r : r + COMP, c : c + COMP] = 0.5 * (same - other)
    for sign in range(2):
        hi, lo = split(full[sign])
        w_ref[sign, 0:BAND, :] = jnp.concatenate([hi[:, 0:BAND], hi[:, 0:BAND]], axis=1)
        w_ref[sign, BAND:, :] = jnp.concatenate([lo[:, 0:BAND], jnp.zeros((BAND, BAND), jnp.bfloat16)], axis=1)

    for slab in range(3):
        base = window_of(neighbour(slab))
        inv = [1.0 / jnp.sqrt(jnp.full((1, NZ), mass_ref[(base + j) & 127], jnp.float32)) for j in range(WIN)]
        if slab == 1:
            load_slab(own_ref, base, inv, u_ref, v0_ref, s_ref, rel_ref)
        else:
            for j in range(WIN):
                at = slab * 2 + j
                inv_ref[at : at + 1, :] = inv[j]


def near_kernel(pay_ref, w_ref, inv_ref, u0, v0, s, rel, u1_ref, u2_ref, v1_ref, sums_ref, u0n, v0n, sn):
    inv = [inv_ref[4 + j : 5 + j, :] for j in range(WIN)]
    offset = (1 - lax.axis_index("core")) * PAY_PAD
    load_slab(pay_ref, window_of(neighbour(2)), inv, u0n, v0n, sn, offset=offset)
    moments = Moments(rel, v0)
    lanes_of = [slice(p * NZ, (p + 1) * NZ) for p in range(NP)]
    for x in range(CX):
        moments.add(0, x, {p: cell_rows(v0, x, lanes_of[p]) for p in range(NP)})

    def first(plane):
        return (u0, plane - 3) if plane < 6 else (u0n, plane - 6)

    def scales_of(plane):
        return cell_rows(s, plane - 3, ALL) if plane < 6 else cell_rows(sn, plane - 6, ALL)

    for pair in range(NP // 2):
        for plane in (4, 5, 6, 7):
            scales, fields = scales_of(plane), {}
            for q, g in enumerate(stencil(w_ref, [first(plane + d) for d in (-1, 0, 1)], pair)):
                p = 2 * pair + q
                lanes = lanes_of[p]
                v = fields[p] = [scales[y] * g[y] for y in range(NY)]
                store_scaled(u1_ref, slice((plane - 4) * PAD, (plane - 3) * PAD), lanes, scales, v)
                if plane < 6:
                    for y in range(NY):
                        at = (plane - 4) * ROWS + y * PAD
                        v1_ref[at : at + PAD, lanes] = v[y]
            if plane < 6:
                moments.add(1, plane - 3, fields)
    for pair in range(NP // 2):
        for plane in (5, 6):
            scales, fields = scales_of(plane), {}
            for q, g in enumerate(stencil(w_ref, [(u1_ref, plane - 4 + d) for d in (-1, 0, 1)], pair)):
                p = 2 * pair + q
                lanes = lanes_of[p]
                before = cell_rows(v0, 2, lanes) if plane == 5 else cell_rows(v0n, 0, lanes)
                v = fields[p] = [2.0 * (scales[y] * g[y]) - before[y] for y in range(NY)]
                store_scaled(u2_ref, slice((plane - 5) * PAD, (plane - 4) * PAD), lanes, scales, v)
            if plane == 5:
                moments.add(2, 2, fields)
    for n in range(4):
        for j in range(WIN):
            at = (n * WIN + j) * 8
            sums_ref[at : at + 8, :] = moments.sums.get((n, j), jnp.zeros((8, NZ), jnp.float32))


def far_kernel(
    pay_ref, w_ref, inv_ref, u0, v0, s, rel, u1, u2, v1, sums_ref, out_ref, pm_ref, u0f, v0f, sf, u1f, u2f, v1f, result, sems
):
    inv = [inv_ref[j : j + 1, :] for j in range(WIN)]
    load_slab(pay_ref, window_of(neighbour(0)), inv, u0f, v0f, sf)
    moments = Moments(rel, v0)
    for n in range(4):
        for j in range(WIN):
            at = (n * WIN + j) * 8
            moments.sums[n, j] = sums_ref[at : at + 8, :]
    lanes_of = [slice(p * NZ, (p + 1) * NZ) for p in range(NP)]

    def source(step, plane):
        if step == 0:
            return (u0f, plane) if plane < 3 else (u0, plane - 3)
        if step == 1:
            return (u1f, plane - 1) if plane < 4 else (u1, plane - 4)
        return (u2f, plane - 2) if plane < 5 else (u2, plane - 5)

    writes = []
    for step in range(3):
        for pair, plane in [(pair, plane) for pair in range(NP // 2) for plane in range(step + 1, step + 4)]:
            own = plane >= 3
            scales = cell_rows(s, plane - 3, ALL) if own else cell_rows(sf, plane, ALL)
            fields = {}
            planes = [source(step, plane + d) for d in (-1, 0, 1)]
            for q, g in enumerate(stencil(w_ref, planes, pair)):
                p = 2 * pair + q
                lanes = lanes_of[p]
                v = [scales[y] * g[y] for y in range(NY)]
                if step == 1:
                    before = cell_rows(v0, plane - 3, lanes) if own else cell_rows(v0f, plane, lanes)
                    v = [2.0 * v[y] - before[y] for y in range(NY)]
                elif step == 2:
                    before = cell_rows(v1f, 0, lanes) if plane == 3 else cell_rows(v1, plane - 4, lanes)
                    v = [2.0 * v[y] - before[y] for y in range(NY)]
                fields[p] = v
                if step == 0 and own:
                    for y in range(NY):
                        v1f[y * PAD : (y + 1) * PAD, lanes] = v[y]
                if step < 2:
                    at = plane - 1 - step
                    store_scaled((u1f, u2f)[step], slice(at * PAD, (at + 1) * PAD), lanes, scales, v)
                else:
                    for y in range(NY):
                        result[plane - 3, pl.ds(p * NY + y, COMP, stride=NP * NY), :] = v[y][0:COMP]
            if step == 2 and pair == NP // 2 - 1:
                x = plane - 3
                write = pltpu.make_async_copy(
                    result.at[x].reshape(COMP * NP, NY, NZ), out_ref.at[:, turned(x)], sems.at[x]
                )
                write.start()
                writes.append(write)
            if own:
                moments.add(step + 1, plane - 3, fields)

    lane = lax.broadcasted_iota(jnp.int32, (4, NZ), 1)
    total = jnp.zeros((4, NZ), jnp.float32)
    for j in range(WIN):
        stacked = jnp.concatenate([jnp.sum(moments.sums[n, j], axis=0, keepdims=True) for n in range(4)], axis=0)
        value = jnp.sum(stacked, axis=1, keepdims=True)
        total = total + jnp.where(lane == ((window_of(own_index()) + j) & 127), value, 0.0)
    pm_ref[...] = jnp.broadcast_to(total[None], pm_ref.shape)
    for write in writes:
        write.wait()


HBM = pl.BlockSpec(memory_space=pltpu.HBM)
VMEM = pl.BlockSpec(memory_space=pltpu.VMEM)
SMEM = pl.BlockSpec(memory_space=pltpu.SMEM)


def body(site_class, probe_signs, masses, force_blocks):
    payload = pl.pallas_call(
        payload_kernel,
        out_shape=pltpu.VMEM((PAY_PAD, NZ), jnp.int32),
        in_specs=[HBM, HBM],
        out_specs=VMEM,
        scratch_shapes=[pltpu.SemaphoreType.DMA((2,))],
        cost_estimate=pl.CostEstimate(flops=0, bytes_accessed=800000, transcendentals=0),
        name="payload",
    )(probe_signs.reshape(COMP * NP * CX, NY, NZ), site_class.reshape(ATOMS * CX, NY, NZ))

    count = 64
    far = lax.ppermute(payload, SPACE, [(i, (i + 1) % count if i % 2 else (i - 1) % count) for i in range(count)])
    slab = HALF + (BAND, WIDE)
    *prepared, again = pl.pallas_call(
        prepare_kernel,
        out_shape=(
            pltpu.VMEM((2, 2 * BAND, 2 * BAND), jnp.bfloat16),
            pltpu.VMEM((8, NZ), jnp.float32),
            pltpu.VMEM(slab, jnp.bfloat16),
            pltpu.VMEM((CX * ROWS, WIDE), jnp.float32),
            pltpu.VMEM((CX * ROWS, NZ), jnp.float32),
            pltpu.VMEM((CX * ROWS, NZ), jnp.int32),
            pltpu.VMEM((2 * PAY_PAD, NZ), jnp.int32),
        ),
        in_specs=[SMEM, VMEM, VMEM],
        out_specs=(VMEM,) * 7,
        scratch_shapes=[pltpu.VMEM((2, BAND, NZ), jnp.float32)],
        cost_estimate=pl.CostEstimate(flops=1000000, bytes_accessed=300000, transcendentals=0),
        name="prepare",
    )(masses, force_blocks, payload)
    near = lax.all_to_all(again, "core", 0, 0, tiled=True)

    shared = pl.pallas_call(
        near_kernel,
        out_shape=(
            pltpu.VMEM(HALF + (4 * PAD, WIDE), jnp.bfloat16),
            pltpu.VMEM(HALF + (2 * PAD, WIDE), jnp.bfloat16),
            pltpu.VMEM((2 * ROWS, WIDE), jnp.float32),
            pltpu.VMEM((16 * 8, NZ), jnp.float32),
        ),
        in_specs=[VMEM] * 7,
        out_specs=(VMEM,) * 4,
        scratch_shapes=[
            pltpu.VMEM(slab, jnp.bfloat16),
            pltpu.VMEM((CX * ROWS, WIDE), jnp.float32),
            pltpu.VMEM((CX * ROWS, NZ), jnp.float32),
        ],
        compiler_params=pltpu.CompilerParams(vmem_limit_bytes=24 * 2**20),
        cost_estimate=pl.CostEstimate(flops=800000000, bytes_accessed=1000000, transcendentals=0),
        name="near_part",
    )(near, *prepared)

    group = 32
    last, parts = pl.pallas_call(
        far_kernel,
        out_shape=(
            jax.ShapeDtypeStruct((COMP * NP, CX, NY, NZ), jnp.float32),
            pltpu.VMEM((group, 4, NZ), jnp.float32),
        ),
        in_specs=[VMEM] * 11,
        out_specs=(HBM, VMEM),
        scratch_shapes=[
            pltpu.VMEM(slab, jnp.bfloat16),
            pltpu.VMEM((CX * ROWS, WIDE), jnp.float32),
            pltpu.VMEM((CX * ROWS, NZ), jnp.float32),
            pltpu.VMEM(slab, jnp.bfloat16),
            pltpu.VMEM(slab, jnp.bfloat16),
            pltpu.VMEM((ROWS, WIDE), jnp.float32),
            pltpu.VMEM((CX, SIGN_ROWS // CX, NZ), jnp.float32),
            pltpu.SemaphoreType.DMA((CX,)),
        ],
        compiler_params=pltpu.CompilerParams(vmem_limit_bytes=24 * 2**20),
        cost_estimate=pl.CostEstimate(flops=1200000000, bytes_accessed=2000000, transcendentals=0),
        name="far_part",
    )(far, *prepared, *shared)

    parts = lax.all_to_all(parts, NEAR, 0, 0, tiled=True).sum(0)
    parts = jnp.broadcast_to(parts[None], (lax.axis_size("z"), 4, NZ))
    moments = lax.all_to_all(parts, "z", 0, 0, tiled=True).sum(0) * (1.0 / 368640)
    return moments, last.reshape(COMP, NP, CX, NY, NZ)


def solution(mesh):
    fine = Mesh(mesh.devices.reshape(2, 16, 2, 2, 4), SPACE + PROBE)
    return jax.shard_map(
        body,
        mesh=fine,
        in_specs=(P(None, SPACE, None, None), P(None, PROBE, SPACE, None, None), P(), P()),
        out_specs=(P(), P(None, PROBE, SPACE, None, None)),
        check_vma=False,
    )
```
